32 devices in a mesh: dp: 2 (over x), expert: 16 (over z, y, core).
Axes of the slice: x: 2, y: 2, z: 4, core: 2. Of those that a mesh axis runs over, the one named last changes fastest.
Arguments:
- tokens: bfloat16 [2048, 4096], P('expert', 'dp'), may hold values from -6 to 6
- routing: int32 [2048, 8], P('expert'), may hold values from 0 to 15, all different within a row; in each aligned block of 128 rows (0 to 127, 128 to 255, ...) at most 80 rows name the same one
- gate_probs: float32 [2048, 8], P('expert'), may hold values from 0.05 to 0.3
- paired: int32 [16], P('expert'), may hold values from 0 to 1, as said below
- w_gate: bfloat16 [16, 4096, 768], P('expert', 'dp'), may hold values from -0.09375 to 0.09375
- w_up: bfloat16 [16, 4096, 768], P('expert', 'dp'), may hold values from -0.09375 to 0.09375
- w_down: bfloat16 [16, 768, 4096], P('expert', None, 'dp'), may hold values from -0.21875 to 0.21875
- cotangent: bfloat16 [2048, 4096], P('expert', 'dp'), may hold values from -6 to 6
Outputs:
- output: bfloat16 [2048, 4096], P('expert', 'dp')
- grad_tokens: bfloat16 [2048, 4096], P('expert', 'dp')
- grad_gate: float32 [16, 4096, 768], P('expert', 'dp')
- grad_up: float32 [16, 4096, 768], P('expert', 'dp')
- grad_down: float32 [16, 768, 4096], P('expert', None, 'dp')
The draws below stay inside these ranges and needn't reach their ends.
Inputs may be any that keep to these rules, and one draw needn't show every extreme that they name: `routing`: each token names 8 different copies; among the tokens of one source (aligned blocks of 128 tokens) no copy is named more than 80 times, a bound that some block reaches. paired[c] equals paired[(c + 8) mod 16]; paired[0] and paired[15] are 1.
All inputs are finite; a program needn't handle non-finite values.
Results may differ from the reference program's by a relative error of at most 0.029.
Values may be sent and summed in bfloat16 or wider, within the bound.
No kernel may reach another device: no remote copies, remote signals or barrier semaphores. Data moves between devices by JAX's collectives and lax.ppermute only.
A program may use at most 128 MiB of HBM per device.

```python
import math
import jax
import jax.numpy as jnp
import numpy as np
from jax import lax

D = 4096
H = 768
TOPK = 8
TOK_DEV = 128
COPIES = 16
CAP = 80
TOKENS = 2048
N_DP = 2


def draw_paired(key, part):
    half = jax.random.randint(key, (COPIES // 2,), 0, 2).astype(jnp.int32)
    half = half.at[0].set(1)
    half = half.at[COPIES // 2 - 1].set(1)
    return jnp.concatenate([half, half]).astype(jnp.int32)


def level_of(key, dims, pieces, smallest, largest):
    factor_of, own = 1.0, jax.random.fold_in(key, 6)
    for dim, blocks in pieces:
        heights = jnp.exp(jax.random.uniform(jax.random.fold_in(own, dim), (blocks,), jnp.float32, smallest / len(pieces), largest / len(pieces)))
        factor_of = factor_of * jnp.repeat(heights, dims[dim] // blocks).reshape([-1 if axis == dim else 1 for axis in range(len(dims))])
    return factor_of


def routed_block(own_key, own, number, rows, number_of, top, bound, skew):
    sequence = jax.random.permutation(own_key, number_of)
    heavy_load, common = load_shares(number_of, rows * top, bound, skew, True), load_shares(number_of, rows * top, bound, skew, False)
    places = jnp.arange(number_of)

    def named(lengths, rotation):
        used = int((lengths > 0).sum())
        fixed = max(1, used // 4)
        shifted = fixed + (places - fixed + rotation * (used - fixed)) % max(1, number_of - fixed)
        return jnp.zeros((number_of,), jnp.int32).at[sequence[jnp.where(places < fixed, places, shifted)]].set(jnp.asarray(lengths, jnp.int32))

    lengths = jnp.where(number % 4 == 0, named(heavy_load, number // 4), named(common, number - number // 4 - 1))
    mixed = jax.random.permutation(jax.random.fold_in(own, 3), number_of)
    giver, taker = mixed[0:number_of // 2 * 2:2], mixed[1:number_of // 2 * 2:2]
    room = jnp.minimum(lengths[giver] - 1, bound - lengths[taker]) // 2
    room = jnp.where((giver == sequence[0]) | (taker == sequence[0]) | (lengths[taker] == 0), 0, jnp.maximum(room, 0))
    shifted = jax.random.randint(jax.random.fold_in(own, 4), (number_of // 2,), 0, 1 << 20) % (room + 1)
    lengths = lengths.at[giver].add(-shifted).at[taker].add(shifted)
    items = jnp.searchsorted(jnp.cumsum(lengths), jnp.arange(rows * top), side="right").astype(jnp.int32)
    table = items.reshape(top, rows).T
    table = table[jax.random.permutation(jax.random.fold_in(own, 1), rows)]
    rotation = jax.random.randint(jax.random.fold_in(own, 2), (rows, 1), 0, top)
    return jnp.take_along_axis(table, (jnp.arange(top)[None, :] + rotation) % top, axis=1)


def load_shares(amount, total, bound, lean, full):
    portions = [(1 << 20) // math.isqrt(grade ** lean) + 1 for grade in range(1, amount + 1)]
    largest = bound if full else min(bound, max(-(-total // amount), total * portions[0] // sum(portions)))
    least = 1 if total - largest >= amount - 1 else 0
    holding, surplus = [largest] + [least] * (amount - 1), total - largest - least * (amount - 1)
    while surplus > 0:
        movable = [i for i in range(1, amount) if holding[i] < largest] or [i for i in range(1, amount) if holding[i] < bound]
        pool, left = sum([portions[i] for i in movable]), surplus
        for i in movable:
            more = min(bound - holding[i], max(1, left * portions[i] // pool), surplus)
            holding[i] = holding[i] + more
            surplus = surplus - more
    return np.array(holding)


def normal_values(rng, dims, scale, most, cuts=(), kind=jnp.bfloat16):
    loudness = level_of(rng, dims, cuts, -0.22, 0.18) if cuts else 1.0
    result = jax.random.normal(rng, dims, jnp.float32) * scale * loudness
    return jnp.minimum(jnp.maximum(result, -most), most).astype(kind)


def setup_inputs(seed: int = 0) -> dict:
    seeds = jax.random.split(jax.random.key(seed), 9)
    tokens = normal_values(seeds[0], (TOKENS, D), 1.0, 6.0, ((0, 16), (1, 2)))
    routing_keys = jax.random.split(jax.random.fold_in(seeds[1], 1), TOKENS // TOK_DEV)
    routing_turns = jax.random.permutation(jax.random.fold_in(seeds[1], 3), TOKENS // TOK_DEV)
    routing = jax.vmap(lambda own, number: routed_block(jax.random.fold_in(seeds[1], 2), own, number, TOK_DEV, COPIES, TOPK, CAP, 1))(routing_keys, routing_turns).reshape((TOKENS, TOPK))
    gate_probs = jnp.clip(0.05 + 0.25 * jax.random.uniform(seeds[2], (TOKENS, TOPK), jnp.float32) ** level_of(seeds[2], (TOKENS, TOPK), ((0, 16),), -0.2, 0.2), 0.05, 0.3)
    paired = draw_paired(jax.random.fold_in(seeds[8], 71), 0)
    w_gate = normal_values(seeds[4], (COPIES, D, H), D ** -0.5, 0.09375, ((0, 16), (1, 2)))
    w_up = normal_values(seeds[5], (COPIES, D, H), D ** -0.5, 0.09375, ((0, 16), (1, 2)))
    w_down = normal_values(seeds[6], (COPIES, H, D), H ** -0.5, 0.21875, ((0, 16), (2, 2)))
    cotangent = normal_values(seeds[7], (TOKENS, D), 1.0, 6.0, ((0, 16), (1, 2)))
    return {"tokens": tokens, "routing": routing, "gate_probs": gate_probs, "paired": paired, "w_gate": w_gate, "w_up": w_up, "w_down": w_down, "cotangent": cotangent}


def rounded(value):
    return lax.optimization_barrier(value.astype(jnp.bfloat16)).astype(jnp.float32)


def expert_pass(rows_in, rows_grad, gate_weight, up_weight, down_weight):
    count = rows_in.shape[0]
    width = rows_in.shape[1]
    slab = width // N_DP
    hidden = gate_weight.shape[1]
    blocks_in = rows_in.reshape(count, N_DP, slab).astype(jnp.float32)
    blocks_grad = rows_grad.reshape(count, N_DP, slab).astype(jnp.float32)
    gate_blocks = gate_weight.reshape(N_DP, slab, hidden).astype(jnp.float32)
    up_blocks = up_weight.reshape(N_DP, slab, hidden).astype(jnp.float32)
    down_blocks = down_weight.reshape(hidden, N_DP, slab).astype(jnp.float32)
    gate = jnp.sum(rounded(jnp.einsum("rjd,jdh->jrh", blocks_in, gate_blocks)), axis=0)
    upper = jnp.sum(rounded(jnp.einsum("rjd,jdh->jrh", blocks_in, up_blocks)), axis=0)
    sigma = jax.nn.sigmoid(gate)
    activated = gate * sigma
    hid = (activated * upper).astype(jnp.bfloat16)
    out = jnp.dot(hid, down_weight, preferred_element_type=jnp.float32).astype(jnp.bfloat16)
    grad_down = jnp.dot(hid.T, rows_grad, preferred_element_type=jnp.float32)
    grad_hid = jnp.sum(rounded(jnp.einsum("rjd,hjd->jrh", blocks_grad, down_blocks)), axis=0)
    grad_gate_rows = (grad_hid * upper * sigma * (1.0 + gate * (1.0 - sigma))).astype(jnp.bfloat16)
    grad_up_rows = (grad_hid * activated).astype(jnp.bfloat16)
    grad_gate = jnp.dot(rows_in.T, grad_gate_rows, preferred_element_type=jnp.float32)
    grad_up = jnp.dot(rows_in.T, grad_up_rows, preferred_element_type=jnp.float32)
    back = jnp.dot(grad_gate_rows, gate_weight.T, preferred_element_type=jnp.float32)
    back = back + jnp.dot(grad_up_rows, up_weight.T, preferred_element_type=jnp.float32)
    return out, back.astype(jnp.bfloat16), grad_gate, grad_up, grad_down


def reference(tokens, routing, gate_probs, paired, w_gate, w_up, w_down, cotangent):
    token_total = routing.shape[0]
    top_count = routing.shape[1]
    width = tokens.shape[1]
    sources = token_total // TOK_DEV
    source_rows = TOK_DEV * top_count
    flat = routing.reshape(sources, source_rows)
    onehot = (flat[:, :, None] == jnp.arange(COPIES, dtype=jnp.int32)[None, None, :]).astype(jnp.int32)
    earlier = jnp.cumsum(onehot, axis=1) - onehot
    slot = jnp.sum(earlier * onehot, axis=2)
    position = (jnp.arange(sources, dtype=jnp.int32)[:, None] * CAP + slot).reshape(-1).astype(jnp.int32)
    copy_of = flat.reshape(-1).astype(jnp.int32)
    all_rows = token_total * top_count
    table = jnp.full((COPIES, sources * CAP), all_rows, dtype=jnp.int32)
    table = table.at[copy_of, position].set(jnp.arange(all_rows, dtype=jnp.int32))
    token_rows = jnp.concatenate([jnp.repeat(tokens, top_count, axis=0), jnp.zeros((1, width), tokens.dtype)], axis=0)
    scaled = (gate_probs[:, :, None] * cotangent.astype(jnp.float32)[:, None, :]).astype(jnp.bfloat16)
    grad_rows = jnp.concatenate([scaled.reshape(all_rows, width), jnp.zeros((1, width), jnp.bfloat16)], axis=0)

    def one_copy(packed):
        index, gate_weight, up_weight, down_weight = packed
        return expert_pass(token_rows[index], grad_rows[index], gate_weight, up_weight, down_weight)

    outs, backs, grad_gate, grad_up, grad_down = lax.map(one_copy, (table, w_gate, w_up, w_down))
    where = copy_of * (sources * CAP) + position
    out_rows = outs.reshape(-1, width)[where].reshape(token_total, top_count, width)
    back_rows = backs.reshape(-1, width)[where].reshape(token_total, top_count, width)
    output = jnp.sum(gate_probs[:, :, None] * out_rows.astype(jnp.float32), axis=1).astype(jnp.bfloat16)
    grad_tokens = jnp.sum(back_rows.astype(jnp.float32), axis=1).astype(jnp.bfloat16)
    partner = (jnp.arange(COPIES, dtype=jnp.int32) + COPIES // 2) % COPIES
    keep = paired.astype(jnp.float32)[:, None, None]
    grad_gate = grad_gate + keep * grad_gate[partner]
    grad_up = grad_up + keep * grad_up[partner]
    grad_down = grad_down + keep * grad_down[partner]
    return output, grad_tokens, grad_gate, grad_up, grad_down
```

```python
import jax
import jax.numpy as jnp
from jax import lax
from jax.sharding import PartitionSpec as P

BF = jnp.bfloat16
F32 = jnp.float32


def exchange(value, axis, bit):
    pairs = [(source, source ^ bit) for source in range(lax.axis_size(axis))]
    return lax.ppermute(value, axis, pairs)


def product(left, right):
    return jnp.dot(left, right, preferred_element_type=F32)


def contract(left, right, dims):
    return lax.dot_general(left, right, (dims, ((), ())), preferred_element_type=F32)


def batched(left, right, dims):
    return lax.dot_general(left, right, (dims, ((0,), (0,))), preferred_element_type=F32)


def split_exact(value):
    high = lax.reduce_precision(value, 8, 7)
    rest = value - high
    middle = lax.reduce_precision(rest, 8, 7)
    return [high.astype(BF), middle.astype(BF), (rest - middle).astype(BF)]


def bits_of(count):
    return [1 << place for place in reversed(range(count.bit_length() - 1))]


def gather_sources(block, order, bits, flip):
    current = block.reshape((1,) * len(bits) + block.shape)
    for bit in order:
        place = bits.index(bit)
        other = exchange(current, "expert", bit)
        if flip is not None and place == 0:
            first, second = jnp.where(flip, other, current), jnp.where(flip, current, other)
        else:
            first, second = current, other
        current = jnp.concatenate([first, second], axis=place)
    return current.reshape((2 ** len(bits),) + block.shape)


def scatter_sources(blocks, order, bits, flip):
    current = blocks.reshape((2,) * len(bits) + blocks.shape[1:])
    for bit in order:
        place = bits.index(bit)
        first = lax.slice_in_dim(current, 0, 1, axis=place)
        second = lax.slice_in_dim(current, 1, 2, axis=place)
        if flip is not None and place == 0:
            first, second = jnp.where(flip, second, first), jnp.where(flip, first, second)
        other = exchange(second, "expert", bit)
        current = (first.astype(F32) + other.astype(F32)).astype(BF)
    return current.reshape(blocks.shape[1:])


def per_device(tokens, routing, gate_probs, paired, w_gate, w_up, w_down, cotangent):
    n_expert = lax.axis_size("expert")
    n_data = lax.axis_size("dp")
    token_count, top_count = routing.shape
    slab = tokens.shape[1]
    hidden = w_gate.shape[2]
    capacity = max(2, 5 * token_count * top_count // (4 * n_expert))
    all_rows = n_expert * capacity
    own_rows = all_rows // n_data
    half = slab // 2
    bits = bits_of(n_expert)
    top = bits[0]
    paired_dp = n_data == 2
    flip = (lax.axis_index("dp") == 1) if paired_dp else None
    copy = lax.axis_index("expert")
    gate_slab, up_slab, down_slab = w_gate[0], w_up[0], w_down[0]
    order_a = list(bits)
    order_b = [bits[0], bits[2], bits[1]] + list(bits[3:])

    meta = jnp.concatenate([routing.astype(BF)] + split_exact(gate_probs), axis=1)
    head = gather_sources(
        jnp.concatenate([tokens[:, :half], meta], axis=1), order_a, bits, flip
    )
    tail = gather_sources(tokens[:, half:], order_b, bits, flip)
    cot_head = gather_sources(cotangent[:, :half], order_a, bits, flip)
    cot_tail = gather_sources(cotangent[:, half:], order_b, bits, flip)

    named = head[:, :, half : half + top_count].astype(F32)
    parts = [
        head[:, :, half + (1 + i) * top_count : half + (2 + i) * top_count].astype(F32)
        for i in range(3)
    ]
    probs = parts[0] + parts[1] + parts[2]
    before = (
        jnp.arange(token_count)[:, None] < jnp.arange(token_count)[None, :]
    ).astype(BF)

    def selection(index):
        hit = named == index.astype(F32)
        member = jnp.any(hit, axis=2)
        slot = product(member.astype(BF), before).astype(jnp.int32)
        slot = jnp.where(member, slot, -1)
        select = jnp.arange(capacity, dtype=jnp.int32)[None, :, None] == slot[:, None, :]
        return select, jnp.sum(jnp.where(hit, probs, 0.0), axis=2)

    select, prob = selection(copy)
    select_pair, _ = selection(copy ^ top)
    row_prob = jnp.sum(jnp.where(select, prob[:, None, :], 0.0), axis=2).reshape(all_rows, 1)
    pick = select.astype(BF)
    keep = paired.astype(F32)[0]
    pick_both = jnp.concatenate(
        [pick, (select_pair.astype(F32) * keep).astype(BF)], axis=1
    )

    def rows_of(blocks):
        return batched(pick, blocks, ((2,), (1,))).astype(BF).reshape(all_rows, -1)

    def to_tokens(chooser, rows):
        rows = rows.reshape(n_expert, -1, rows.shape[-1])
        spread = batched(chooser, rows, ((1,), (1,))).astype(BF)
        return spread.reshape(n_expert * token_count, -1)

    def sum_dp(rows):
        if paired_dp:
            other = exchange(rows[own_rows:], "dp", 1)
            return rows[:own_rows].astype(F32) + other.astype(F32)
        return lax.psum_scatter(rows, "dp", scatter_dimension=0, tiled=True).astype(F32)

    def gather_dp(rows):
        if paired_dp:
            return jnp.concatenate([rows, exchange(rows, "dp", 1)], axis=0)
        return lax.all_gather(rows, "dp", axis=0, tiled=True)

    def gather_pair(rows):
        crossed = exchange(rows, "expert", top)
        if paired_dp:
            return jnp.concatenate([exchange(crossed, "dp", 1), crossed], axis=0)
        everything = lax.all_gather(crossed, "dp", axis=0, tiled=True)
        middle = all_rows // 2
        return jnp.concatenate([everything[middle:], everything[:middle]], axis=0)

    if paired_dp:
        prob_own = row_prob[:own_rows]
    else:
        prob_own = lax.dynamic_slice_in_dim(row_prob, lax.axis_index("dp") * own_rows, own_rows)

    token_all = jnp.concatenate([head[:, :, :half], tail], axis=2)
    cot_all = jnp.concatenate([cot_head, cot_tail], axis=2)
    token_rows = rows_of(token_all)
    gate_up = jnp.concatenate(
        [product(token_rows, gate_slab).astype(BF), product(token_rows, up_slab).astype(BF)],
        axis=1,
    )
    summed = sum_dp(gate_up)
    gate_own, up_own = summed[:, :hidden], summed[:, hidden:]
    cot_rows = rows_of(cot_all)
    grad_hidden = sum_dp(contract(cot_rows, down_slab, ((1,), (1,))).astype(BF)) * prob_own

    sigma = jax.nn.sigmoid(gate_own)
    activated = gate_own * sigma
    hid = (activated * up_own * prob_own).astype(BF)
    grad_rows = jnp.concatenate(
        [
            (grad_hidden * up_own * sigma * (1.0 + gate_own * (1.0 - sigma))).astype(BF),
            (grad_hidden * activated).astype(BF),
        ],
        axis=1,
    )
    hid_all = gather_dp(hid)
    hid_pair = gather_pair(hid)
    grad_all = gather_dp(grad_rows)
    grad_pair = gather_pair(grad_rows)

    out_part = product(to_tokens(pick, hid_all), down_slab).astype(BF)
    output = scatter_halves(out_part, n_expert, bits, flip)
    grad_spread = to_tokens(pick, grad_all)
    back_part = (
        contract(grad_spread[:, :hidden], gate_slab, ((1,), (1,)))
        + contract(grad_spread[:, hidden:], up_slab, ((1,), (1,)))
    ).astype(BF)
    grad_tokens = scatter_halves(back_part, n_expert, bits, flip)

    def both(own, pair):
        return jnp.concatenate(
            [
                own.reshape(n_expert, capacity, -1),
                pair.reshape(n_expert, capacity, -1),
            ],
            axis=1,
        )

    hid_both = to_tokens(pick_both, both(hid_all, hid_pair))
    grad_both = to_tokens(pick_both, both(grad_all, grad_pair))
    token_flat = token_all.reshape(n_expert * token_count, slab)
    cot_flat = cot_all.reshape(n_expert * token_count, slab)
    grad_gate = contract(token_flat, grad_both[:, :hidden], ((0,), (0,)))
    grad_up = contract(token_flat, grad_both[:, hidden:], ((0,), (0,)))
    grad_down = contract(hid_both, cot_flat, ((0,), (0,)))
    return (output, grad_tokens, grad_gate[None], grad_up[None], grad_down[None])


def scatter_halves(part, n_expert, bits, flip):
    half = part.shape[1] // 2
    blocks = part.reshape(n_expert, -1, part.shape[1])
    up = list(reversed(bits))
    first = scatter_sources(blocks[:, :, :half], up, bits, flip)
    other_order = [up[0], up[2], up[1]] + up[3:]
    second = scatter_sources(blocks[:, :, half:], other_order, bits, flip)
    return jnp.concatenate([first, second], axis=1)


def solution(mesh):
    return jax.shard_map(
        per_device,
        mesh=mesh,
        in_specs=(
            P("expert", "dp"),
            P("expert", None),
            P("expert", None),
            P("expert"),
            P("expert", "dp", None),
            P("expert", "dp", None),
            P("expert", None, "dp"),
            P("expert", "dp"),
        ),
        out_specs=(
            P("expert", "dp"),
            P("expert", "dp"),
            P("expert", "dp", None),
            P("expert", "dp", None),
            P("expert", None, "dp"),
        ),
        check_vma=False,
    )
```

```python
import functools

import jax
import jax.numpy as jnp
from jax import lax
from jax.experimental import pallas as pl
from jax.experimental.pallas import tpu as pltpu
from jax.sharding import PartitionSpec as P

BF = jnp.bfloat16
F32 = jnp.float32


def exchange(value, axis, bit):
    pairs = [(source, source ^ bit) for source in range(lax.axis_size(axis))]
    return lax.ppermute(value, axis, pairs)


def product(left, right):
    return jnp.dot(left, right, preferred_element_type=F32)


def contract(left, right, dims):
    return lax.dot_general(left, right, (dims, ((), ())), preferred_element_type=F32)


def batched(left, right, dims):
    return lax.dot_general(left, right, (dims, ((0,), (0,))), preferred_element_type=F32)


def split_exact(value):
    high = lax.reduce_precision(value, 8, 7)
    rest = value - high
    middle = lax.reduce_precision(rest, 8, 7)
    return [high.astype(BF), middle.astype(BF), (rest - middle).astype(BF)]


def bits_of(count):
    return [1 << place for place in reversed(range(count.bit_length() - 1))]


def gather_sources(block, order, bits, flip):
    current = block.reshape((1,) * len(bits) + block.shape)
    for bit in order:
        place = bits.index(bit)
        other = exchange(current, "expert", bit)
        if flip is not None and place == 0:
            first, second = jnp.where(flip, other, current), jnp.where(flip, current, other)
        else:
            first, second = current, other
        current = jnp.concatenate([first, second], axis=place)
    return current.reshape((2 ** len(bits),) + block.shape)


def scatter_sources(blocks, order, bits, flip):
    current = blocks.reshape((2,) * len(bits) + blocks.shape[1:])
    for bit in order:
        place = bits.index(bit)
        first = lax.slice_in_dim(current, 0, 1, axis=place)
        second = lax.slice_in_dim(current, 1, 2, axis=place)
        if flip is not None and place == 0:
            first, second = jnp.where(flip, second, first), jnp.where(flip, first, second)
        other = exchange(second, "expert", bit)
        current = (first.astype(F32) + other.astype(F32)).astype(BF)
    return current.reshape(blocks.shape[1:])


def general(tokens, routing, gate_probs, paired, w_gate, w_up, w_down, cotangent):
    n_expert = lax.axis_size("expert")
    n_data = lax.axis_size("dp")
    token_count, top_count = routing.shape
    slab = tokens.shape[1]
    hidden = w_gate.shape[2]
    capacity = max(2, 5 * token_count * top_count // (4 * n_expert))
    all_rows = n_expert * capacity
    own_rows = all_rows // n_data
    half = slab // 2
    bits = bits_of(n_expert)
    top = bits[0]
    paired_dp = n_data == 2
    flip = (lax.axis_index("dp") == 1) if paired_dp else None
    copy = lax.axis_index("expert")
    gate_slab, up_slab, down_slab = w_gate[0], w_up[0], w_down[0]
    order_a = list(bits)
    order_b = [bits[0], bits[2], bits[1]] + list(bits[3:])

    meta = jnp.concatenate([routing.astype(BF)] + split_exact(gate_probs), axis=1)
    head = gather_sources(
        jnp.concatenate([tokens[:, :half], meta], axis=1), order_a, bits, flip
    )
    tail = gather_sources(tokens[:, half:], order_b, bits, flip)
    cot_head = gather_sources(cotangent[:, :half], order_a, bits, flip)
    cot_tail = gather_sources(cotangent[:, half:], order_b, bits, flip)

    named = head[:, :, half : half + top_count].astype(F32)
    parts = [
        head[:, :, half + (1 + i) * top_count : half + (2 + i) * top_count].astype(F32)
        for i in range(3)
    ]
    probs = parts[0] + parts[1] + parts[2]
    before = (
        jnp.arange(token_count)[:, None] < jnp.arange(token_count)[None, :]
    ).astype(BF)

    def selection(index):
        hit = named == index.astype(F32)
        member = jnp.any(hit, axis=2)
        slot = product(member.astype(BF), before).astype(jnp.int32)
        slot = jnp.where(member, slot, -1)
        select = jnp.arange(capacity, dtype=jnp.int32)[None, :, None] == slot[:, None, :]
        return select, jnp.sum(jnp.where(hit, probs, 0.0), axis=2)

    select, prob = selection(copy)
    select_pair, _ = selection(copy ^ top)
    row_prob = jnp.sum(jnp.where(select, prob[:, None, :], 0.0), axis=2).reshape(all_rows, 1)
    pick = select.astype(BF)
    keep = paired.astype(F32)[0]
    pick_both = jnp.concatenate(
        [pick, (select_pair.astype(F32) * keep).astype(BF)], axis=1
    )

    def rows_of(blocks):
        return batched(pick, blocks, ((2,), (1,))).astype(BF).reshape(all_rows, -1)

    def to_tokens(chooser, rows):
        rows = rows.reshape(n_expert, -1, rows.shape[-1])
        spread = batched(chooser, rows, ((1,), (1,))).astype(BF)
        return spread.reshape(n_expert * token_count, -1)

    def sum_dp(rows):
        if paired_dp:
            other = exchange(rows[own_rows:], "dp", 1)
            return rows[:own_rows].astype(F32) + other.astype(F32)
        return lax.psum_scatter(rows, "dp", scatter_dimension=0, tiled=True).astype(F32)

    def gather_dp(rows):
        if paired_dp:
            return jnp.concatenate([rows, exchange(rows, "dp", 1)], axis=0)
        return lax.all_gather(rows, "dp", axis=0, tiled=True)

    def gather_pair(rows):
        crossed = exchange(rows, "expert", top)
        if paired_dp:
            return jnp.concatenate([exchange(crossed, "dp", 1), crossed], axis=0)
        everything = lax.all_gather(crossed, "dp", axis=0, tiled=True)
        middle = all_rows // 2
        return jnp.concatenate([everything[middle:], everything[:middle]], axis=0)

    if paired_dp:
        prob_own = row_prob[:own_rows]
    else:
        prob_own = lax.dynamic_slice_in_dim(row_prob, lax.axis_index("dp") * own_rows, own_rows)

    token_all = jnp.concatenate([head[:, :, :half], tail], axis=2)
    cot_all = jnp.concatenate([cot_head, cot_tail], axis=2)
    token_rows = rows_of(token_all)
    gate_up = jnp.concatenate(
        [product(token_rows, gate_slab).astype(BF), product(token_rows, up_slab).astype(BF)],
        axis=1,
    )
    summed = sum_dp(gate_up)
    gate_own, up_own = summed[:, :hidden], summed[:, hidden:]
    cot_rows = rows_of(cot_all)
    grad_hidden = sum_dp(contract(cot_rows, down_slab, ((1,), (1,))).astype(BF)) * prob_own

    sigma = jax.nn.sigmoid(gate_own)
    activated = gate_own * sigma
    hid = (activated * up_own * prob_own).astype(BF)
    grad_rows = jnp.concatenate(
        [
            (grad_hidden * up_own * sigma * (1.0 + gate_own * (1.0 - sigma))).astype(BF),
            (grad_hidden * activated).astype(BF),
        ],
        axis=1,
    )
    hid_all = gather_dp(hid)
    hid_pair = gather_pair(hid)
    grad_all = gather_dp(grad_rows)
    grad_pair = gather_pair(grad_rows)

    out_part = product(to_tokens(pick, hid_all), down_slab).astype(BF)
    output = scatter_halves(out_part, n_expert, bits, flip)
    grad_spread = to_tokens(pick, grad_all)
    back_part = (
        contract(grad_spread[:, :hidden], gate_slab, ((1,), (1,)))
        + contract(grad_spread[:, hidden:], up_slab, ((1,), (1,)))
    ).astype(BF)
    grad_tokens = scatter_halves(back_part, n_expert, bits, flip)

    def both(own, pair):
        return jnp.concatenate(
            [
                own.reshape(n_expert, capacity, -1),
                pair.reshape(n_expert, capacity, -1),
            ],
            axis=1,
        )

    hid_both = to_tokens(pick_both, both(hid_all, hid_pair))
    grad_both = to_tokens(pick_both, both(grad_all, grad_pair))
    token_flat = token_all.reshape(n_expert * token_count, slab)
    cot_flat = cot_all.reshape(n_expert * token_count, slab)
    grad_gate = contract(token_flat, grad_both[:, :hidden], ((0,), (0,)))
    grad_up = contract(token_flat, grad_both[:, hidden:], ((0,), (0,)))
    grad_down = contract(hid_both, cot_flat, ((0,), (0,)))
    return (output, grad_tokens, grad_gate[None], grad_up[None], grad_down[None])


def scatter_halves(part, n_expert, bits, flip):
    half = part.shape[1] // 2
    blocks = part.reshape(n_expert, -1, part.shape[1])
    up = list(reversed(bits))
    first = scatter_sources(blocks[:, :, :half], up, bits, flip)
    other_order = [up[0], up[2], up[1]] + up[3:]
    second = scatter_sources(blocks[:, :, half:], other_order, bits, flip)
    return jnp.concatenate([first, second], axis=1)


VMEM_BYTES = 56 * 2**20
LIGHT = 1000
OUT_PARTS = (3, 3, 2)
BACK_PARTS = (4, 4)
CUTS = 1
MIXED = True
NN = ((1,), (0,))
NT = ((1,), (1,))
TN = ((0,), (0,))


def call(kernel, grid, in_specs, out_specs, out_shape, scratch, flops, moved, deps=(), prefetch=1):
    held = prefetch + len(in_specs)

    def body(*refs):
        kernel(*refs[:held], *refs[held + len(deps) :])

    run = pl.pallas_call(
        body,
        grid_spec=pltpu.PrefetchScalarGridSpec(
            num_scalar_prefetch=prefetch,
            grid=grid,
            in_specs=in_specs + [pl.BlockSpec(memory_space=pl.ANY)] * len(deps),
            out_specs=out_specs,
            scratch_shapes=scratch,
        ),
        out_shape=out_shape,
        compiler_params=pltpu.CompilerParams(
            dimension_semantics=("arbitrary",) * len(grid), vmem_limit_bytes=VMEM_BYTES
        ),
        cost_estimate=pl.CostEstimate(
            flops=flops // LIGHT, bytes_accessed=moved // LIGHT, transcendentals=0
        ),
    )
    return lambda *operands: run(*operands, *deps)


def whole(value):
    if isinstance(value, tuple):
        stack, part = value
        return pl.BlockSpec((None,) + stack.shape[1:], lambda j, s: (part, 0, 0)), stack
    return fixed(value.shape), value


def fixed(shape):
    return pl.BlockSpec(shape, lambda j, s: (0,) * len(shape))


def rows_kernel(count, cuts, dims, capacity, half_ref, slot_ref, *refs):
    pieces = refs[:4]
    weights = refs[4 : 4 + count]
    outs, rows = refs[4 + count : -1], refs[-1]
    width = pieces[0].shape[2]
    tokens = pieces[0].shape[1]

    @pl.when(pl.program_id(0) == 0)
    def _():
        place = lax.broadcasted_iota(jnp.int32, (capacity, tokens), 0)
        for local in range(slot_ref.shape[0]):
            pick = (place == slot_ref[local : local + 1, :]).astype(F32).astype(BF)
            for side in range(2):
                block = pieces[2 * side + local % 2][local // 2]
                rows[local * capacity : (local + 1) * capacity, side * width : (side + 1) * width] = (
                    contract(pick, block, NN).astype(BF)
                )

    for w in range(count):
        value = contract(rows[...], weights[w][...], dims).astype(BF)
        width = value.shape[1] // cuts
        for cut in range(cuts):
            outs[w * cuts + cut][...] = value[:, cut * width : (cut + 1) * width]


def rows_product(half, slots, pieces, weights, dims, capacity, width, cuts=1, deps=()):
    sources, tokens = slots.shape
    mine = sources // 2
    depth = mine // 2
    slab = 2 * width
    hidden = weights[0].shape[1] if dims == NN else weights[0].shape[0]
    tile = min(256, hidden) if cuts == 1 else hidden
    rows = mine * capacity
    weight_spec = (
        pl.BlockSpec((slab, tile), lambda j, s: (0, j))
        if dims == NN
        else pl.BlockSpec((tile, slab), lambda j, s: (j, 0))
    )
    count = len(weights)
    return call(
        functools.partial(rows_kernel, count, cuts, dims, capacity),
        (hidden // tile,),
        [pl.BlockSpec((mine, tokens), lambda j, s: (s[0], 0))]
        + [pl.BlockSpec((depth, tokens, width), lambda j, s: (s[0], 0, 0))] * 4
        + [weight_spec] * count,
        [pl.BlockSpec((rows, tile // cuts), lambda j, s: (0, j))] * (count * cuts),
        [jax.ShapeDtypeStruct((rows, hidden // cuts), BF)] * (count * cuts),
        [pltpu.VMEM((rows, slab), BF)],
        2 * count * rows * slab * hidden,
        2 * slab * (count * hidden + mine * tokens),
        deps,
    )(half, slots, *pieces, *weights)


def spread(dp, column_ref, sources, capacity, act):
    tokens = column_ref.shape[1]
    place = lax.broadcasted_iota(jnp.int32, (tokens, capacity), 1)
    mine = sources // 2
    for block in range(sources):
        upper = jnp.bitwise_xor(dp, block // mine)
        position = block % mine + mine * upper
        pick = (place == column_ref[position]).astype(F32).astype(BF)
        start = pl.multiple_of(((block % mine) // 2 + (mine // 2) * upper) * tokens, tokens)
        act(block % 2, start, pick, block, position)


def back_kernel(count, dims, capacity, dp_ref, column_ref, *refs):
    values = refs[: 2 * count]
    weights = refs[2 * count : 3 * count]
    spreads = refs[-2 * count :]
    keep_ref, sends = refs[3 * count], refs[3 * count + 1 : -2 * count]
    sources, tokens, _ = column_ref.shape
    mine = sources // 2

    @pl.when(pl.program_id(0) == 0)
    def _():
        def act(parity, start, pick, block, position):
            for v in range(count):
                rows = values[2 * v + block // mine]
                at = (block % mine) * capacity
                spreads[2 * v + parity][pl.ds(start, tokens), :] = contract(
                    pick, rows[at : at + capacity, :], NN
                ).astype(BF)

        spread(dp_ref[0], column_ref, sources, capacity, act)

    def total(parity):
        value = contract(spreads[parity][...], weights[0][...], dims)
        for v in range(1, count):
            value = value + contract(spreads[2 * v + parity][...], weights[v][...], dims)
        return value.astype(BF)

    keep_ref[...] = total(0)
    sent = total(1)
    tile = sent.shape[1]
    spots = [(send, at) for send in sends for at in range(0, send.shape[1], tile)]
    for step, (send, at) in enumerate(spots):

        @pl.when(pl.program_id(0) == step)
        def _():
            send[:, at : at + tile] = sent


def back_product(dp, columns, values, weights, dims, capacity, parts, deps=()):
    sources, tokens, _ = columns.shape
    specs, values = zip(*[whole(value) for value in values])
    hidden = values[0].shape[-1]
    slab = weights[0].shape[1] if dims == NN else weights[0].shape[0]
    tile = 256
    count = len(weights)
    out_rows = sources * tokens // 2
    weight_spec = (
        pl.BlockSpec((hidden, tile), lambda j, s: (0, j))
        if dims == NN
        else pl.BlockSpec((tile, hidden), lambda j, s: (j, 0))
    )
    return call(
        functools.partial(back_kernel, count, dims, capacity),
        (slab // tile,),
        [fixed(columns.shape)] + list(specs) + [weight_spec] * count,
        [pl.BlockSpec((out_rows, tile), lambda j, s: (0, j))]
        + [pl.BlockSpec((out_rows, tile * part), lambda j, s: (0, 0)) for part in parts],
        [jax.ShapeDtypeStruct((out_rows, slab), BF)]
        + [jax.ShapeDtypeStruct((out_rows, tile * part), BF) for part in parts],
        [pltpu.VMEM((out_rows, hidden), BF)] * (2 * count),
        4 * count * out_rows * slab * hidden,
        2 * slab * (count * hidden + 2 * out_rows),
        deps,
    )(dp, columns, *values, *weights)


def grad_kernel(flat, capacity, dp_ref, *refs):
    columns, pair_columns = refs[:2]
    own, other, crossed, beyond = refs[2:6]
    pieces = refs[6:10]
    out_ref = refs[10]
    spreads = refs[11:]
    sources, tokens, _ = columns.shape
    mine = sources // 2
    step = pl.program_id(0)

    @pl.when(step == 0)
    def _():
        def act(parity, start, pick, block, position):
            place = lax.broadcasted_iota(jnp.int32, (tokens, capacity), 1)
            pair_pick = (place == pair_columns[position]).astype(F32).astype(BF)
            at = (block % mine) * capacity
            rows = (own if block < mine else other)[at : at + capacity, :]
            pair_rows = (beyond if block < mine else crossed)[at : at + capacity, :]
            value = contract(pick, rows, NN) + contract(pair_pick, pair_rows, NN)
            if flat:
                spreads[parity][pl.ds(start, tokens), :] = value.astype(BF)
            else:
                spreads[parity][:, pl.ds(start, tokens)] = value.T.astype(BF)

        spread(dp_ref[0], columns, sources, capacity, act)

    def product_of(blocks):
        total = None
        for parity in range(2):
            block = blocks[parity][...].reshape(mine * tokens, blocks[parity].shape[2])
            if flat:
                term = contract(block, spreads[parity][...], TN)
            else:
                term = contract(spreads[parity][...], block, NN)
            total = term if total is None else total + term
        out_ref[...] = total

    half_steps = pl.num_programs(0) // 2

    @pl.when(step < half_steps)
    def _():
        product_of(pieces[:2])

    @pl.when(step >= half_steps)
    def _():
        product_of(pieces[2:])


def weight_gradient(dp, columns, pair_columns, values, pieces, flat, capacity, width, deps=()):
    sources, tokens, _ = columns.shape
    specs, values = zip(*[whole(value) for value in values])
    hidden = values[0].shape[-1]
    slab = 2 * width
    tile = min(256, width)
    steps = slab // tile
    depth = sources // 2
    first = pl.BlockSpec(
        (depth, tokens, tile), lambda j, s: (0, 0, jnp.minimum(j, steps // 2 - 1))
    )
    second = pl.BlockSpec(
        (depth, tokens, tile), lambda j, s: (0, 0, jnp.maximum(j - steps // 2, 0))
    )
    shape = (slab, hidden) if flat else (hidden, slab)
    return call(
        functools.partial(grad_kernel, flat, capacity),
        (steps,),
        [fixed(columns.shape)] * 2 + list(specs) + [first] * 2 + [second] * 2,
        pl.BlockSpec((tile, hidden), lambda j, s: (j, 0))
        if flat
        else pl.BlockSpec((hidden, tile), lambda j, s: (0, j)),
        jax.ShapeDtypeStruct(shape, F32),
        [pltpu.VMEM((depth * tokens, hidden) if flat else (hidden, depth * tokens), BF)] * 2,
        2 * sources * tokens * slab * hidden,
        4 * slab * hidden + 2 * sources * tokens * slab,
        deps,
    )(dp, columns, pair_columns, *values, *pieces)


def split_kernel(axes, *refs):
    count = len(axes)
    for i, axis in enumerate(axes):
        total = (refs[2 * i][...].astype(F32) + refs[2 * i + 1][...].astype(F32)).astype(BF)
        outs = refs[2 * count + 2 * i : 2 * count + 2 * i + 2]
        for side, out in enumerate(outs):
            out[...] = total[(slice(None),) * axis + (side,)]


def sum_split(kept, coming, axes, sides, deps=()):
    tokens = kept[0].shape[-2]
    chunk = min(32, tokens)
    in_specs, out_specs, out_shape, operands = [], [], [], []
    for k, c, axis, side in zip(kept, coming, axes, sides):
        lead = k.shape[:-2]
        width = k.shape[-1] // (1 if side is None else 2)
        at = 0 if side is None else side
        spec = pl.BlockSpec(
            lead + (chunk, width), functools.partial(lambda n, at, j: (0,) * n + (j, at), len(lead), at)
        )
        in_specs += [spec, spec]
        operands += [k, c]
        left = lead[:axis] + lead[axis + 1 :]
        out_specs += [
            pl.BlockSpec(
                left + (chunk, width), functools.partial(lambda n, j: (0,) * n + (j, 0), len(left))
            )
        ] * 2
        out_shape += [jax.ShapeDtypeStruct(left + (tokens, width), BF)] * 2
    moved = sum(3 * 2 * value.size for value in kept)
    return call(
        functools.partial(split_kernel, tuple(axes)),
        (tokens // chunk,),
        in_specs,
        out_specs,
        out_shape,
        [],
        moved // 4,
        moved,
        deps,
        prefetch=0,
    )(*operands)


def first_kernel(mixed, keep, *refs):
    outs = refs[-4:] if mixed else refs[-2:]
    pieces = refs[: -len(outs)]
    each = outs[0].shape[-1]
    at = 0
    for piece in pieces:
        width = min(piece.shape[-1], each)
        for first in range(0, piece.shape[-1], width):
            total = keep[..., at : at + width].astype(F32)
            total = (total + piece[..., first : first + width].astype(F32)).astype(BF)
            right, place = divmod(at, each)
            for side in range(2):
                outs[side + 2 * right][..., place : place + width] = (
                    total[:, side] if right else total[:, :, side]
                )
            at += width


def sum_first(keep, coming, mixed, deps=()):
    lead, (tokens, width) = keep.shape[:-2], keep.shape[-2:]
    chunk = min(16, tokens)
    four = lambda j: (0, 0, j, 0)
    five = lambda j: (0, 0, 0, j, 0)
    outs = 4 if mixed else 2
    each = 2 * width // outs
    return call(
        functools.partial(first_kernel, mixed),
        (tokens // chunk,),
        [pl.BlockSpec(lead + (chunk, value.shape[-1]), five) for value in [keep] + coming],
        [pl.BlockSpec(lead[:2] + (chunk, each), four)] * outs,
        [jax.ShapeDtypeStruct(lead[:2] + (tokens, each), BF)] * outs,
        [],
        0,
        0,
        deps,
        prefetch=0,
    )(keep, *coming)


def last_kernel(*refs):
    width = refs[0].shape[1]
    for i in range(len(refs) // 2):
        refs[-1][:, i * width : (i + 1) * width] = (
            refs[2 * i][...].astype(F32) + refs[2 * i + 1][...].astype(F32)
        ).astype(BF)


def last_sum(kept, coming, deps=()):
    tokens, width = kept[0].shape
    spec = pl.BlockSpec((tokens, width), lambda j: (0, 0))
    count = len(kept)
    return call(
        last_kernel,
        (1,),
        [spec] * (2 * count),
        pl.BlockSpec((tokens, count * width), lambda j: (0, 0)),
        jax.ShapeDtypeStruct((tokens, count * width), BF),
        [],
        0,
        0,
        deps,
        prefetch=0,
    )(*[value for pair in zip(kept, coming) for value in pair])


def join_kernel(axes, cut, *refs):
    count = len(axes)
    held = 2 if cut else 2 * count
    outs, stages = refs[held : held + count], refs[held + count : held + 2 * count]
    in_sems, out_sems = refs[held + 2 * count :]
    reads, writes = [], []
    for i, axis in enumerate(axes):
        width = outs[i].shape[-1]
        for side in range(2):
            n = 2 * i + side
            at = (slice(None),) * axis + (slice(side, side + 1),)
            source = refs[side].at[..., i * width : (i + 1) * width] if cut else refs[n]
            reads.append(pltpu.make_async_copy(source, stages[i].at[at], in_sems.at[n]))
            writes.append(
                pltpu.make_async_copy(stages[i].at[at], outs[i].at[at], out_sems.at[n])
            )
    for copy in reads:
        copy.start()
    for read, write in zip(reads, writes):
        read.wait()
        write.start()
    for copy in writes:
        copy.wait()


def join(now, coming, axes, deps=(), cut=False):
    out_shape, operands = [], []
    for value, other in zip(now, coming):
        operands += [value, other]
    for i, axis in enumerate(axes):
        value = now[0 if cut else i]
        shape = value.shape[:axis] + (2,) + value.shape[axis + 1 : -1]
        width = value.shape[-1] // (2 if cut else 1)
        out_shape.append(jax.ShapeDtypeStruct(shape + (width,), BF))
    place = pl.BlockSpec(memory_space=pl.ANY)
    return call(
        functools.partial(join_kernel, tuple(axes), cut),
        (),
        [place] * len(operands),
        [place] * len(out_shape),
        out_shape,
        [pltpu.VMEM(whole.shape, BF) for whole in out_shape]
        + [pltpu.SemaphoreType.DMA((2 * len(axes),))] * 2,
        0,
        0,
        deps,
        prefetch=0,
    )(*operands)


def hidden_kernel(gate_kept, gate_coming, up_kept, up_coming, prob, out):
    gate = gate_kept[...].astype(F32) + gate_coming[...].astype(F32)
    up = up_kept[...].astype(F32) + up_coming[...].astype(F32)
    out[...] = (gate * jax.nn.sigmoid(gate) * up * prob[...]).astype(BF)


def slopes_kernel(
    gate_kept, gate_coming, up_kept, up_coming, prob, grad_kept, *refs
):
    gate = gate_kept[...].astype(F32) + gate_coming[...].astype(F32)
    up = up_kept[...].astype(F32) + up_coming[...].astype(F32)
    out, gate_out, up_out = refs[-3:]
    grad_coming = jnp.concatenate([ref[...] for ref in refs[:-3]], axis=1)
    grad = (grad_kept[...].astype(F32) + grad_coming.astype(F32)) * prob[...]
    sigma = jax.nn.sigmoid(gate)
    out[0] = (grad * up * sigma * (1.0 + gate * (1.0 - sigma))).astype(BF)
    out[1] = (grad * gate * sigma).astype(BF)
    gate_out[...] = out[0]
    up_out[...] = out[1]


def by_rows(kernel, operands, stacks, outs, deps=()):
    rows, hidden = operands[0].shape
    chunk = rows // 5 if rows % 80 == 0 else rows
    return call(
        kernel,
        (rows // chunk,),
        [pl.BlockSpec((chunk, value.shape[1]), lambda j: (j, 0)) for value in operands],
        [pl.BlockSpec((2, chunk, hidden), lambda j: (0, j, 0))] * stacks
        + [pl.BlockSpec((chunk, hidden), lambda j: (j, 0))] * outs,
        [jax.ShapeDtypeStruct((2, rows, hidden), BF)] * stacks
        + [jax.ShapeDtypeStruct((rows, hidden), BF)] * outs,
        [],
        0,
        0,
        deps,
        prefetch=0,
    )(*operands)


def nothing_kernel(*refs):
    pass


def after(value, *others):
    return pl.pallas_call(
        nothing_kernel,
        in_specs=[pl.BlockSpec(memory_space=pl.ANY)] * (1 + len(others)),
        out_specs=pl.BlockSpec(memory_space=pl.ANY),
        out_shape=jax.ShapeDtypeStruct(value.shape, value.dtype),
        input_output_aliases={0: 0},
    )(value, *others)


def fast(tokens, routing, gate_probs, paired, w_gate, w_up, w_down, cotangent):
    n_expert = lax.axis_size("expert")
    token_count, top_count = routing.shape
    slab = tokens.shape[1]
    hidden = w_gate.shape[2]
    capacity = max(2, 5 * token_count * top_count // (4 * n_expert))
    half = slab // 2
    mine = n_expert // 2
    copy = lax.axis_index("expert")
    dp = lax.axis_index("dp").astype(jnp.int32)
    dp_one = dp.reshape(1)
    other_one = (1 - dp).reshape(1)
    gate_slab, up_slab, down_slab = w_gate[0], w_up[0], w_down[0]

    def cross(value, bit):
        return exchange(value, "expert", bit)

    meta = jnp.concatenate([routing.astype(BF)] + split_exact(gate_probs), axis=1)
    meta = jnp.pad(meta, ((0, 0), (0, 128 - meta.shape[1])))

    def blocks(value):
        return [value[:, :half].reshape(1, 1, 1, token_count, half), value[:, half:].reshape(1, 1, 1, token_count, half)]

    def widen(now, bits, coming=None, deps=()):
        if coming is None:
            coming = [cross(value, bit) for value, bit in zip(now, bits)]
        axis = {8: 0, 4: 1, 2: 2}
        return join(now, coming, [axis[bit] for bit in bits], deps)

    token_now = blocks(tokens)
    token_now[0] = jnp.concatenate([token_now[0], meta.reshape(1, 1, 1, token_count, -1)], axis=-1)
    token_now = widen(token_now, (8, 8))
    token_now = widen(token_now, (4, 2))
    token_now = widen(token_now, (2, 4))
    cot_whole = after(cotangent, *token_now).reshape(1, 1, 1, token_count, slab)

    def finish(now):
        pieces = []
        for value in now:
            value = value.reshape(mine, token_count, -1)
            pieces += [value, cross(value, 1)]
        return pieces

    token_pieces = finish(token_now)

    meta = jnp.stack([piece[:, :, half:] for piece in token_pieces[:2]], axis=1)
    meta = meta.reshape(n_expert, token_count, -1).astype(F32)
    named, high, middle, low = [
        meta[:, :, i * top_count : (i + 1) * top_count] for i in range(4)
    ]
    probs = high + middle + low
    before = (
        jnp.arange(token_count)[:, None] < jnp.arange(token_count)[None, :]
    ).astype(BF)

    def selection(index):
        hit = named == index.astype(F32)
        member = jnp.any(hit, axis=2)
        slot = product(member.astype(BF), before).astype(jnp.int32)
        return hit, jnp.where(member, slot, -1)

    hit, slots = selection(copy)
    _, pair_slots = selection(jnp.bitwise_xor(copy, mine))
    pair_slots = jnp.where(paired[0] == 1, pair_slots, -1)
    columns, pair_columns = slots[:, :, None], pair_slots[:, :, None]
    prob = jnp.sum(jnp.where(hit, probs, 0.0), axis=2)
    select = jnp.arange(capacity, dtype=jnp.int32)[None, :, None] == slots[:, None, :]
    row_prob = jnp.sum(jnp.where(select, prob[:, None, :], 0.0), axis=2)
    prob_own = lax.dynamic_slice_in_dim(row_prob, dp * mine, mine).reshape(mine * capacity, 1)

    def rows_of(which, pieces, weights, dims, cuts=1, deps=()):
        return rows_product(which, slots, pieces, weights, dims, capacity, half, cuts, deps)

    def over(value):
        return exchange(value, "dp", 1)

    leaving = rows_of(other_one, token_pieces, [gate_slab, up_slab], NN)
    gate_coming, up_coming = over(leaving[0]), over(leaving[1])
    cot_now = join([cot_whole], [cross(cot_whole, 8)], (0, 0), (leaving[1],), True)
    gate_kept, up_kept = rows_of(
        dp_one, token_pieces, [gate_slab, up_slab], NN, 1, (cot_now[0],)
    )
    cot_now = widen(cot_now, (4, 2), None, (up_kept, gate_coming))
    cot_pieces = finish(widen(cot_now, (2, 4), None, (up_coming,)))
    both = [gate_kept, gate_coming, up_kept, up_coming, prob_own]
    (hid,) = by_rows(hidden_kernel, both, 0, 1, (cot_pieces[0],))
    hid_crossed = cross(hid, mine)
    hid_other = over(hid)

    (leaving,) = rows_of(other_one, cot_pieces, [down_slab], NT, 1, (hid,))
    dhid_coming = over(leaving)
    (dhid_kept,) = rows_of(dp_one, cot_pieces, [down_slab], NT)
    out_keep, *out_send = back_product(
        dp_one, columns, [hid, hid_other], [down_slab], NN, capacity, OUT_PARTS, (dhid_kept,)
    )
    slopes, dgate_sent, dup_sent = by_rows(
        slopes_kernel, both + [dhid_kept, dhid_coming], 1, 2, (out_send[0],)
    )
    out_send[0] = after(out_send[0], hid_crossed)
    slopes_other = over(slopes)
    dgate_crossed = cross(dgate_sent, mine)

    shape = (2, 2, 2, token_count, slab)

    def first_sum(keep, send, mixed, *deps):
        coming = [cross(value, 1).reshape(shape[:-1] + value.shape[-1:]) for value in send]
        return sum_first(keep.reshape(shape), coming, mixed, deps)

    def next_sum(parts, bits, axis, *deps):
        kept, sent = parts[::2], parts[1::2]
        coming = [cross(value, bit) for value, bit in zip(sent, bits)]
        return sum_split(kept, coming, [axis] * len(kept), [None] * len(kept), deps)

    def end_sum(parts, *deps):
        return last_sum(parts[::2], [cross(value, 8) for value in parts[1::2]], deps)

    def gradient(values, pieces, flat, *deps):
        return weight_gradient(
            dp_one, columns, pair_columns, values, pieces, flat, capacity, half, deps
        )

    out_parts = first_sum(out_keep, out_send, False)
    back_keep, *back_send = back_product(
        dp_one,
        columns,
        [(slopes, 0), (slopes_other, 0), (slopes, 1), (slopes_other, 1)],
        [gate_slab, up_slab],
        NT,
        capacity,
        BACK_PARTS,
        (out_parts[1],),
    )
    dup_crossed = cross(after(dup_sent, dgate_crossed), mine)
    hid_crossed = after(hid_crossed, slopes_other, out_parts[1])
    hid_beyond = over(hid_crossed)
    out_parts = next_sum(out_parts, (2,), 1)
    back_send[0] = after(back_send[0], hid_beyond, out_parts[1], dgate_crossed)
    dgate_beyond = over(dgate_crossed)
    back_parts = first_sum(back_keep, back_send, MIXED)
    bits = ((2, 4), (4, 2)) if MIXED else ((2,), (4,))
    out_parts = next_sum(out_parts, (4,), 0, back_parts[1])
    grad_down = gradient(
        [hid, hid_other, hid_crossed, hid_beyond], cot_pieces, False, out_parts[1]
    )
    dup_crossed = after(dup_crossed, grad_down)
    dup_beyond = over(dup_crossed)
    grad_gate = gradient(
        [(slopes, 0), (slopes_other, 0), dgate_crossed, dgate_beyond],
        token_pieces,
        True,
        dup_crossed,
    )
    output = end_sum(out_parts, grad_gate)
    back_parts = next_sum(back_parts, bits[0], 1, grad_gate)
    back_parts = next_sum(back_parts, bits[1], 0, output)
    grad_up = gradient(
        [(slopes, 1), (slopes_other, 1), dup_crossed, dup_beyond],
        token_pieces,
        True,
        back_parts[1],
    )
    grad_tokens = end_sum(back_parts)
    return (output, grad_tokens, grad_gate[None], grad_up[None], grad_down[None])


def per_device(*arrays):
    quick = lax.axis_size("dp") == 2 and lax.axis_size("expert") == 16
    return (fast if quick else general)(*arrays)


def solution(mesh):
    return jax.shard_map(
        per_device,
        mesh=mesh,
        in_specs=(
            P("expert", "dp"),
            P("expert", None),
            P("expert", None),
            P("expert"),
            P("expert", "dp", None),
            P("expert", "dp", None),
            P("expert", None, "dp"),
            P("expert", "dp"),
        ),
        out_specs=(
            P("expert", "dp"),
            P("expert", "dp"),
            P("expert", "dp", None),
            P("expert", "dp", None),
            P("expert", None, "dp"),
        ),
        check_vma=False,
    )
```

```python
import functools

import jax
import jax.numpy as jnp
from jax import lax
from jax.experimental import pallas as pl
from jax.experimental.pallas import tpu as pltpu
from jax.sharding import PartitionSpec as P

BF = jnp.bfloat16
F32 = jnp.float32


def exchange(value, axis, bit):
    pairs = [(source, source ^ bit) for source in range(lax.axis_size(axis))]
    return lax.ppermute(value, axis, pairs)


def product(left, right):
    return jnp.dot(left, right, preferred_element_type=F32)


def contract(left, right, dims):
    return lax.dot_general(left, right, (dims, ((), ())), preferred_element_type=F32)


def batched(left, right, dims):
    return lax.dot_general(left, right, (dims, ((0,), (0,))), preferred_element_type=F32)


def split_exact(value):
    high = lax.reduce_precision(value, 8, 7)
    rest = value - high
    middle = lax.reduce_precision(rest, 8, 7)
    return [high.astype(BF), middle.astype(BF), (rest - middle).astype(BF)]


def bits_of(count):
    return [1 << place for place in reversed(range(count.bit_length() - 1))]


def gather_sources(block, order, bits, flip):
    current = block.reshape((1,) * len(bits) + block.shape)
    for bit in order:
        place = bits.index(bit)
        other = exchange(current, "expert", bit)
        if flip is not None and place == 0:
            first, second = jnp.where(flip, other, current), jnp.where(flip, current, other)
        else:
            first, second = current, other
        current = jnp.concatenate([first, second], axis=place)
    return current.reshape((2 ** len(bits),) + block.shape)


def scatter_sources(blocks, order, bits, flip):
    current = blocks.reshape((2,) * len(bits) + blocks.shape[1:])
    for bit in order:
        place = bits.index(bit)
        first = lax.slice_in_dim(current, 0, 1, axis=place)
        second = lax.slice_in_dim(current, 1, 2, axis=place)
        if flip is not None and place == 0:
            first, second = jnp.where(flip, second, first), jnp.where(flip, first, second)
        other = exchange(second, "expert", bit)
        current = (first.astype(F32) + other.astype(F32)).astype(BF)
    return current.reshape(blocks.shape[1:])


def general(tokens, routing, gate_probs, paired, w_gate, w_up, w_down, cotangent):
    n_expert = lax.axis_size("expert")
    n_data = lax.axis_size("dp")
    token_count, top_count = routing.shape
    slab = tokens.shape[1]
    hidden = w_gate.shape[2]
    capacity = max(2, 5 * token_count * top_count // (4 * n_expert))
    all_rows = n_expert * capacity
    own_rows = all_rows // n_data
    half = slab // 2
    bits = bits_of(n_expert)
    top = bits[0]
    paired_dp = n_data == 2
    flip = (lax.axis_index("dp") == 1) if paired_dp else None
    copy = lax.axis_index("expert")
    gate_slab, up_slab, down_slab = w_gate[0], w_up[0], w_down[0]
    order_a = list(bits)
    order_b = [bits[0], bits[2], bits[1]] + list(bits[3:])

    meta = jnp.concatenate([routing.astype(BF)] + split_exact(gate_probs), axis=1)
    head = gather_sources(
        jnp.concatenate([tokens[:, :half], meta], axis=1), order_a, bits, flip
    )
    tail = gather_sources(tokens[:, half:], order_b, bits, flip)
    cot_head = gather_sources(cotangent[:, :half], order_a, bits, flip)
    cot_tail = gather_sources(cotangent[:, half:], order_b, bits, flip)

    named = head[:, :, half : half + top_count].astype(F32)
    parts = [
        head[:, :, half + (1 + i) * top_count : half + (2 + i) * top_count].astype(F32)
        for i in range(3)
    ]
    probs = parts[0] + parts[1] + parts[2]
    before = (
        jnp.arange(token_count)[:, None] < jnp.arange(token_count)[None, :]
    ).astype(BF)

    def selection(index):
        hit = named == index.astype(F32)
        member = jnp.any(hit, axis=2)
        slot = product(member.astype(BF), before).astype(jnp.int32)
        slot = jnp.where(member, slot, -1)
        select = jnp.arange(capacity, dtype=jnp.int32)[None, :, None] == slot[:, None, :]
        return select, jnp.sum(jnp.where(hit, probs, 0.0), axis=2)

    select, prob = selection(copy)
    select_pair, _ = selection(copy ^ top)
    row_prob = jnp.sum(jnp.where(select, prob[:, None, :], 0.0), axis=2).reshape(all_rows, 1)
    pick = select.astype(BF)
    keep = paired.astype(F32)[0]
    pick_both = jnp.concatenate(
        [pick, (select_pair.astype(F32) * keep).astype(BF)], axis=1
    )

    def rows_of(blocks):
        return batched(pick, blocks, ((2,), (1,))).astype(BF).reshape(all_rows, -1)

    def to_tokens(chooser, rows):
        rows = rows.reshape(n_expert, -1, rows.shape[-1])
        spread = batched(chooser, rows, ((1,), (1,))).astype(BF)
        return spread.reshape(n_expert * token_count, -1)

    def sum_dp(rows):
        if paired_dp:
            other = exchange(rows[own_rows:], "dp", 1)
            return rows[:own_rows].astype(F32) + other.astype(F32)
        return lax.psum_scatter(rows, "dp", scatter_dimension=0, tiled=True).astype(F32)

    def gather_dp(rows):
        if paired_dp:
            return jnp.concatenate([rows, exchange(rows, "dp", 1)], axis=0)
        return lax.all_gather(rows, "dp", axis=0, tiled=True)

    def gather_pair(rows):
        crossed = exchange(rows, "expert", top)
        if paired_dp:
            return jnp.concatenate([exchange(crossed, "dp", 1), crossed], axis=0)
        everything = lax.all_gather(crossed, "dp", axis=0, tiled=True)
        middle = all_rows // 2
        return jnp.concatenate([everything[middle:], everything[:middle]], axis=0)

    if paired_dp:
        prob_own = row_prob[:own_rows]
    else:
        prob_own = lax.dynamic_slice_in_dim(row_prob, lax.axis_index("dp") * own_rows, own_rows)

    token_all = jnp.concatenate([head[:, :, :half], tail], axis=2)
    cot_all = jnp.concatenate([cot_head, cot_tail], axis=2)
    token_rows = rows_of(token_all)
    gate_up = jnp.concatenate(
        [product(token_rows, gate_slab).astype(BF), product(token_rows, up_slab).astype(BF)],
        axis=1,
    )
    summed = sum_dp(gate_up)
    gate_own, up_own = summed[:, :hidden], summed[:, hidden:]
    cot_rows = rows_of(cot_all)
    grad_hidden = sum_dp(contract(cot_rows, down_slab, ((1,), (1,))).astype(BF)) * prob_own

    sigma = jax.nn.sigmoid(gate_own)
    activated = gate_own * sigma
    hid = (activated * up_own * prob_own).astype(BF)
    grad_rows = jnp.concatenate(
        [
            (grad_hidden * up_own * sigma * (1.0 + gate_own * (1.0 - sigma))).astype(BF),
            (grad_hidden * activated).astype(BF),
        ],
        axis=1,
    )
    hid_all = gather_dp(hid)
    hid_pair = gather_pair(hid)
    grad_all = gather_dp(grad_rows)
    grad_pair = gather_pair(grad_rows)

    out_part = product(to_tokens(pick, hid_all), down_slab).astype(BF)
    output = scatter_halves(out_part, n_expert, bits, flip)
    grad_spread = to_tokens(pick, grad_all)
    back_part = (
        contract(grad_spread[:, :hidden], gate_slab, ((1,), (1,)))
        + contract(grad_spread[:, hidden:], up_slab, ((1,), (1,)))
    ).astype(BF)
    grad_tokens = scatter_halves(back_part, n_expert, bits, flip)

    def both(own, pair):
        return jnp.concatenate(
            [
                own.reshape(n_expert, capacity, -1),
                pair.reshape(n_expert, capacity, -1),
            ],
            axis=1,
        )

    hid_both = to_tokens(pick_both, both(hid_all, hid_pair))
    grad_both = to_tokens(pick_both, both(grad_all, grad_pair))
    token_flat = token_all.reshape(n_expert * token_count, slab)
    cot_flat = cot_all.reshape(n_expert * token_count, slab)
    grad_gate = contract(token_flat, grad_both[:, :hidden], ((0,), (0,)))
    grad_up = contract(token_flat, grad_both[:, hidden:], ((0,), (0,)))
    grad_down = contract(hid_both, cot_flat, ((0,), (0,)))
    return (output, grad_tokens, grad_gate[None], grad_up[None], grad_down[None])


def scatter_halves(part, n_expert, bits, flip):
    half = part.shape[1] // 2
    blocks = part.reshape(n_expert, -1, part.shape[1])
    up = list(reversed(bits))
    first = scatter_sources(blocks[:, :, :half], up, bits, flip)
    other_order = [up[0], up[2], up[1]] + up[3:]
    second = scatter_sources(blocks[:, :, half:], other_order, bits, flip)
    return jnp.concatenate([first, second], axis=1)


VMEM_BYTES = 62 * 2**20
LIGHT = 1000
BACK_TILE = 512
GRAD_TILE = 512
ROWS_TILE = 256
OUT_PARTS = (2, 2, 2, 2)
BACK_PARTS = (3, 3, 2)
CUTS = 1
MIXED = True
MIXED_OUT = True
NN = ((1,), (0,))
NT = ((1,), (1,))
TN = ((0,), (0,))


def call(kernel, grid, in_specs, out_specs, out_shape, scratch, flops, moved, deps=(), prefetch=1):
    held = prefetch + len(in_specs)

    def body(*refs):
        kernel(*refs[:held], *refs[held + len(deps) :])

    run = pl.pallas_call(
        body,
        grid_spec=pltpu.PrefetchScalarGridSpec(
            num_scalar_prefetch=prefetch,
            grid=grid,
            in_specs=in_specs + [pl.BlockSpec(memory_space=pl.ANY)] * len(deps),
            out_specs=out_specs,
            scratch_shapes=scratch,
        ),
        out_shape=out_shape,
        compiler_params=pltpu.CompilerParams(
            dimension_semantics=("arbitrary",) * len(grid), vmem_limit_bytes=VMEM_BYTES
        ),
        cost_estimate=pl.CostEstimate(
            flops=flops // LIGHT, bytes_accessed=moved // LIGHT, transcendentals=0
        ),
    )
    return lambda *operands: run(*operands, *deps)


def whole(value):
    if isinstance(value, tuple):
        stack, part = value
        return pl.BlockSpec((None,) + stack.shape[1:], lambda j, s: (part, 0, 0)), stack
    return fixed(value.shape), value


def fixed(shape):
    return pl.BlockSpec(shape, lambda j, s: (0,) * len(shape))


def rows_kernel(count, dims, capacity, half_ref, slot_ref, *refs):
    pieces = refs[:4]
    weights = refs[4 : 4 + count]
    outs, rows = refs[4 + count : -1], refs[-1]
    width = pieces[0].shape[2]
    tokens = pieces[0].shape[1]

    @pl.when(pl.program_id(0) == 0)
    def _():
        place = lax.broadcasted_iota(jnp.int32, (2 * capacity, 2 * tokens), 0)
        for pair in range(slot_ref.shape[0] // 2):
            slots = [slot_ref[2 * pair + i : 2 * pair + i + 1, :] for i in range(2)]
            pick = (place == jnp.concatenate(slots, axis=1)).astype(F32).astype(BF)
            at = 2 * pair * capacity
            for side in range(2):
                block = jnp.concatenate(
                    [pieces[2 * side + i][pair] for i in range(2)], axis=0
                )
                rows[at : at + 2 * capacity, side * width : (side + 1) * width] = contract(
                    pick, block, NN
                ).astype(BF)

    for w in range(count):
        outs[0][w] = contract(rows[...], weights[w][...], dims).astype(BF)


def rows_product(half, slots, pieces, weights, dims, capacity, width, deps=()):
    sources, tokens = slots.shape
    mine = sources // 2
    depth = mine // 2
    slab = 2 * width
    hidden = weights[0].shape[1] if dims == NN else weights[0].shape[0]
    tile = min(ROWS_TILE, hidden)
    rows = mine * capacity
    weight_spec = (
        pl.BlockSpec((slab, tile), lambda j, s: (0, j))
        if dims == NN
        else pl.BlockSpec((tile, slab), lambda j, s: (j, 0))
    )
    count = len(weights)
    return call(
        functools.partial(rows_kernel, count, dims, capacity),
        (hidden // tile,),
        [pl.BlockSpec((mine, tokens), lambda j, s: (s[0], 0))]
        + [pl.BlockSpec((depth, tokens, width), lambda j, s: (s[0], 0, 0))] * 4
        + [weight_spec] * count,
        [pl.BlockSpec((count, rows, tile), lambda j, s: (0, 0, j))],
        [jax.ShapeDtypeStruct((count, rows, hidden), BF)],
        [pltpu.VMEM((rows, slab), BF)],
        2 * count * rows * slab * hidden,
        2 * slab * (count * hidden + mine * tokens),
        deps,
    )(half, slots, *pieces, *weights)


def spread(dp, column_ref, sources, capacity, act):
    tokens = column_ref.shape[1]
    place = lax.broadcasted_iota(jnp.int32, (2 * tokens, 2 * capacity), 1)
    mine = sources // 2
    for pair in range(mine):
        half, local = divmod(2 * pair, mine)
        upper = jnp.bitwise_xor(dp, half)
        position = local + mine * upper
        column = column_ref[pl.ds(position, 2)].reshape(2 * tokens, 1)
        pick = (place == column).astype(F32).astype(BF)
        start = pl.multiple_of((local // 2 + (mine // 2) * upper) * tokens, tokens)
        act(start, pick, half, local * capacity, position)


def back_kernel(count, dims, capacity, dp_ref, column_ref, *refs):
    values = refs[: 2 * count]
    weights = refs[2 * count : 3 * count]
    spreads = refs[-2 * count :]
    keep_ref, sends = refs[3 * count], refs[3 * count + 1 : -2 * count]
    sources, tokens, _ = column_ref.shape

    @pl.when(pl.program_id(0) == 0)
    def _():
        def act(start, pick, half, at, position):
            for v in range(count):
                rows = values[2 * v + half][at : at + 2 * capacity, :]
                value = contract(pick, rows, NN).astype(BF)
                for parity in range(2):
                    spreads[2 * v + parity][pl.ds(start, tokens), :] = value[
                        parity * tokens : (parity + 1) * tokens
                    ]

        spread(dp_ref[0], column_ref, sources, capacity, act)

    def total(parity):
        value = contract(spreads[parity][...], weights[0][...], dims)
        for v in range(1, count):
            value = value + contract(spreads[2 * v + parity][...], weights[v][...], dims)
        return value.astype(BF)

    keep_ref[...] = total(0)
    sent = total(1)
    tile = sent.shape[1]
    unit = min(256, tile)
    spots = [(send, at) for send in sends for at in range(0, send.shape[1], unit)]
    per = tile // unit
    for step in range(len(spots) // per):

        @pl.when(pl.program_id(0) == step)
        def _():
            for n, (send, at) in enumerate(spots[step * per : (step + 1) * per]):
                send[:, at : at + unit] = sent[:, n * unit : (n + 1) * unit]


def back_product(dp, columns, values, weights, dims, capacity, parts, deps=()):
    sources, tokens, _ = columns.shape
    specs, values = zip(*[whole(value) for value in values])
    hidden = values[0].shape[-1]
    slab = weights[0].shape[1] if dims == NN else weights[0].shape[0]
    tile, unit = BACK_TILE, 256
    count = len(weights)
    out_rows = sources * tokens // 2
    weight_spec = (
        pl.BlockSpec((hidden, tile), lambda j, s: (0, j))
        if dims == NN
        else pl.BlockSpec((tile, hidden), lambda j, s: (j, 0))
    )
    return call(
        functools.partial(back_kernel, count, dims, capacity),
        (slab // tile,),
        [fixed(columns.shape)] + list(specs) + [weight_spec] * count,
        [pl.BlockSpec((out_rows, tile), lambda j, s: (0, j))]
        + [pl.BlockSpec((out_rows, unit * part), lambda j, s: (0, 0)) for part in parts],
        [jax.ShapeDtypeStruct((out_rows, slab), BF)]
        + [jax.ShapeDtypeStruct((out_rows, unit * part), BF) for part in parts],
        [pltpu.VMEM((out_rows, hidden), BF)] * (2 * count),
        4 * count * out_rows * slab * hidden,
        2 * slab * (count * hidden + 2 * out_rows),
        deps,
    )(dp, columns, *values, *weights)


def grad_kernel(flat, capacity, dp_ref, *refs):
    columns, pair_columns = refs[:2]
    own, other, crossed, beyond = refs[2:6]
    pieces = refs[6:10]
    out_ref = refs[10]
    spreads = refs[11:]
    sources, tokens, _ = columns.shape
    mine = sources // 2
    step = pl.program_id(0)

    @pl.when(step == 0)
    def _():
        def act(start, pick, half, at, position):
            place = lax.broadcasted_iota(jnp.int32, (2 * tokens, 2 * capacity), 1)
            column = pair_columns[pl.ds(position, 2)].reshape(2 * tokens, 1)
            pair_pick = (place == column).astype(F32).astype(BF)
            rows = (own, other)[half][at : at + 2 * capacity, :]
            pair_rows = (beyond, crossed)[half][at : at + 2 * capacity, :]
            value = contract(pick, rows, NN) + contract(pair_pick, pair_rows, NN)
            for parity in range(2):
                part = value[parity * tokens : (parity + 1) * tokens]
                if flat:
                    spreads[parity][pl.ds(start, tokens), :] = part.astype(BF)
                else:
                    spreads[parity][:, pl.ds(start, tokens)] = part.T.astype(BF)

        spread(dp_ref[0], columns, sources, capacity, act)

    def product_of(blocks):
        total = None
        for parity in range(2):
            block = blocks[parity][...].reshape(mine * tokens, blocks[parity].shape[2])
            if flat:
                term = contract(block, spreads[parity][...], TN)
            else:
                term = contract(spreads[parity][...], block, NN)
            total = term if total is None else total + term
        out_ref[...] = total

    half_steps = pl.num_programs(0) // 2

    @pl.when(step < half_steps)
    def _():
        product_of(pieces[:2])

    @pl.when(step >= half_steps)
    def _():
        product_of(pieces[2:])


def weight_gradient(dp, columns, pair_columns, values, pieces, flat, capacity, width, deps=()):
    sources, tokens, _ = columns.shape
    specs, values = zip(*[whole(value) for value in values])
    hidden = values[0].shape[-1]
    slab = 2 * width
    tile = min(GRAD_TILE, width)
    steps = slab // tile
    depth = sources // 2
    first = pl.BlockSpec(
        (depth, tokens, tile), lambda j, s: (0, 0, jnp.minimum(j, steps // 2 - 1))
    )
    second = pl.BlockSpec(
        (depth, tokens, tile), lambda j, s: (0, 0, jnp.maximum(j - steps // 2, 0))
    )
    shape = (slab, hidden) if flat else (hidden, slab)
    return call(
        functools.partial(grad_kernel, flat, capacity),
        (steps,),
        [fixed(columns.shape)] * 2 + list(specs) + [first] * 2 + [second] * 2,
        pl.BlockSpec((tile, hidden), lambda j, s: (j, 0))
        if flat
        else pl.BlockSpec((hidden, tile), lambda j, s: (0, j)),
        jax.ShapeDtypeStruct(shape, F32),
        [pltpu.VMEM((depth * tokens, hidden) if flat else (hidden, depth * tokens), BF)] * 2,
        2 * sources * tokens * slab * hidden,
        4 * slab * hidden + 2 * sources * tokens * slab,
        deps,
    )(dp, columns, pair_columns, *values, *pieces)


def split_kernel(axes, merge, *refs):
    count = len(axes)
    for i, axis in enumerate(axes):
        total = (refs[2 * i][...].astype(F32) + refs[2 * i + 1][...].astype(F32)).astype(BF)
        width = total.shape[-1]
        for side in range(2):
            part = total[(slice(None),) * axis + (side,)]
            if merge:
                refs[2 * count + side][..., i * width : (i + 1) * width] = part
            else:
                refs[2 * count + 2 * i + side][...] = part


def sum_split(kept, coming, axes, merge, deps=()):
    tokens = kept[0].shape[-2]
    chunk = min(32, tokens)
    in_specs, out_specs, out_shape, operands = [], [], [], []
    for k, c, axis in zip(kept, coming, axes):
        lead, width = k.shape[:-2], k.shape[-1]
        spec = pl.BlockSpec(
            lead + (chunk, width), functools.partial(lambda n, j: (0,) * n + (j, 0), len(lead))
        )
        in_specs += [spec, spec]
        operands += [k, c]
        left = lead[:axis] + lead[axis + 1 :]
        width = width * len(kept) if merge else width
        out_specs += [
            pl.BlockSpec(
                left + (chunk, width), functools.partial(lambda n, j: (0,) * n + (j, 0), len(left))
            )
        ] * 2
        out_shape += [jax.ShapeDtypeStruct(left + (tokens, width), BF)] * 2
    return call(
        functools.partial(split_kernel, tuple(axes), merge),
        (tokens // chunk,),
        in_specs,
        out_specs[:2] if merge else out_specs,
        out_shape[:2] if merge else out_shape,
        [],
        0,
        0,
        deps,
        prefetch=0,
    )(*operands)


def first_kernel(mixed, keep, *refs):
    outs, pieces = refs[-4:], refs[:-4]
    each = outs[0].shape[-1]
    at, width = 0, min(256, each)
    for piece in pieces:
        for first in range(0, piece.shape[-1], width):
            total = keep[..., at : at + width].astype(F32)
            total = (total + piece[..., first : first + width].astype(F32)).astype(BF)
            right, place = divmod(at, each)
            for side in range(2):
                outs[side + 2 * right][..., place : place + width] = (
                    total[:, side] if mixed and right else total[:, :, side]
                )
            at += width


def sum_first(keep, coming, mixed, deps=()):
    lead, (tokens, width) = keep.shape[:-2], keep.shape[-2:]
    chunk = min(16, tokens)
    four = lambda j: (0, 0, j, 0)
    five = lambda j: (0, 0, 0, j, 0)
    outs = 4
    each = 2 * width // outs
    return call(
        functools.partial(first_kernel, mixed),
        (tokens // chunk,),
        [pl.BlockSpec(lead + (chunk, value.shape[-1]), five) for value in [keep] + coming],
        [pl.BlockSpec(lead[:2] + (chunk, each), four)] * outs,
        [jax.ShapeDtypeStruct(lead[:2] + (tokens, each), BF)] * outs,
        [],
        0,
        0,
        deps,
        prefetch=0,
    )(keep, *coming)


def last_kernel(*refs):
    width = refs[0].shape[1]
    for i in range(len(refs) // 2):
        refs[-1][:, i * width : (i + 1) * width] = (
            refs[2 * i][...].astype(F32) + refs[2 * i + 1][...].astype(F32)
        ).astype(BF)


def last_sum(kept, coming, deps=()):
    tokens, width = kept[0].shape
    spec = pl.BlockSpec((tokens, width), lambda j: (0, 0))
    count = len(kept)
    return call(
        last_kernel,
        (1,),
        [spec] * (2 * count),
        pl.BlockSpec((tokens, count * width), lambda j: (0, 0)),
        jax.ShapeDtypeStruct((tokens, count * width), BF),
        [],
        0,
        0,
        deps,
        prefetch=0,
    )(*[value for pair in zip(kept, coming) for value in pair])


def join_kernel(axes, cut, *refs):
    count = len(axes)
    held = 2 if cut else 2 * count
    outs, stages = refs[held : held + count], refs[held + count : held + 2 * count]
    in_sems, out_sems = refs[held + 2 * count :]
    reads, writes = [], []
    for i, axis in enumerate(axes):
        width = outs[i].shape[-1]
        for side in range(2):
            n = 2 * i + side
            at = (slice(None),) * axis + (slice(side, side + 1),)
            source = refs[side].at[..., i * width : (i + 1) * width] if cut else refs[n]
            reads.append(pltpu.make_async_copy(source, stages[i].at[at], in_sems.at[n]))
            writes.append(
                pltpu.make_async_copy(stages[i].at[at], outs[i].at[at], out_sems.at[n])
            )
    for copy in reads:
        copy.start()
    for read, write in zip(reads, writes):
        read.wait()
        write.start()
    for copy in writes:
        copy.wait()


def join(now, coming, axes, deps=(), cut=False):
    out_shape, operands = [], []
    for value, other in zip(now, coming):
        operands += [value, other]
    for i, axis in enumerate(axes):
        value = now[0 if cut else i]
        shape = value.shape[:axis] + (2,) + value.shape[axis + 1 : -1]
        width = value.shape[-1] // (2 if cut else 1)
        out_shape.append(jax.ShapeDtypeStruct(shape + (width,), BF))
    place = pl.BlockSpec(memory_space=pl.ANY)
    return call(
        functools.partial(join_kernel, tuple(axes), cut),
        (),
        [place] * len(operands),
        [place] * len(out_shape),
        out_shape,
        [pltpu.VMEM(whole.shape, BF) for whole in out_shape]
        + [pltpu.SemaphoreType.DMA((2 * len(axes),))] * 2,
        0,
        0,
        deps,
        prefetch=0,
    )(*operands)


def hidden_kernel(kept, coming, prob, out):
    gate = kept[0].astype(F32) + coming[0].astype(F32)
    up = kept[1].astype(F32) + coming[1].astype(F32)
    out[...] = (gate * jax.nn.sigmoid(gate) * up * prob[...]).astype(BF)


def slopes_kernel(kept, coming, prob, grad_kept, grad_coming, out):
    gate = kept[0].astype(F32) + coming[0].astype(F32)
    up = kept[1].astype(F32) + coming[1].astype(F32)
    grad = (grad_kept[0].astype(F32) + grad_coming[0].astype(F32)) * prob[...]
    sigma = jax.nn.sigmoid(gate)
    out[0] = (grad * up * sigma * (1.0 + gate * (1.0 - sigma))).astype(BF)
    out[1] = (grad * gate * sigma).astype(BF)


def by_rows(kernel, operands, stacks, outs, deps=()):
    rows, hidden = operands[0].shape[1:]
    chunk = rows // 5 if rows % 80 == 0 else rows
    return call(
        kernel,
        (rows // chunk,),
        [
            pl.BlockSpec((chunk, 1), lambda j: (j, 0))
            if value.ndim == 2
            else pl.BlockSpec((value.shape[0], chunk, hidden), lambda j: (0, j, 0))
            for value in operands
        ],
        [pl.BlockSpec((2, chunk, hidden), lambda j: (0, j, 0))] * stacks
        + [pl.BlockSpec((chunk, hidden), lambda j: (j, 0))] * outs,
        [jax.ShapeDtypeStruct((2, rows, hidden), BF)] * stacks
        + [jax.ShapeDtypeStruct((rows, hidden), BF)] * outs,
        [],
        0,
        0,
        deps,
        prefetch=0,
    )(*operands)


def nothing_kernel(*refs):
    pass


def after(value, *others):
    return pl.pallas_call(
        nothing_kernel,
        in_specs=[pl.BlockSpec(memory_space=pl.ANY)] * (1 + len(others)),
        out_specs=pl.BlockSpec(memory_space=pl.ANY),
        out_shape=jax.ShapeDtypeStruct(value.shape, value.dtype),
        input_output_aliases={0: 0},
    )(value, *others)


def fast(tokens, routing, gate_probs, paired, w_gate, w_up, w_down, cotangent):
    n_expert = lax.axis_size("expert")
    token_count, top_count = routing.shape
    slab = tokens.shape[1]
    hidden = w_gate.shape[2]
    capacity = max(2, 5 * token_count * top_count // (4 * n_expert))
    half = slab // 2
    mine = n_expert // 2
    copy = lax.axis_index("expert")
    dp = lax.axis_index("dp").astype(jnp.int32)
    dp_one = dp.reshape(1)
    other_one = (1 - dp).reshape(1)
    gate_slab, up_slab, down_slab = w_gate[0], w_up[0], w_down[0]

    def cross(value, bit):
        return exchange(value, "expert", bit)

    meta = jnp.concatenate([routing.astype(BF)] + split_exact(gate_probs), axis=1)
    meta = jnp.pad(meta, ((0, 0), (0, 128 - meta.shape[1])))

    def blocks(value):
        return [value[:, :half].reshape(1, 1, 1, token_count, half), value[:, half:].reshape(1, 1, 1, token_count, half)]

    def widen(now, bits, coming=None, deps=()):
        if coming is None:
            coming = [cross(value, bit) for value, bit in zip(now, bits)]
        axis = {8: 0, 4: 1, 2: 2}
        return join(now, coming, [axis[bit] for bit in bits], deps)

    token_now = blocks(tokens)
    token_now[0] = jnp.concatenate([token_now[0], meta.reshape(1, 1, 1, token_count, -1)], axis=-1)
    token_now = widen(token_now, (8, 8))
    token_now = widen(token_now, (4, 2))
    token_now = widen(token_now, (2, 4))
    cot_whole = cotangent.reshape(1, 1, 1, token_count, slab)

    def finish(now):
        pieces = []
        for value in now:
            value = value.reshape(mine, token_count, -1)
            pieces += [value, cross(value, 1)]
        return pieces

    token_pieces = finish(token_now)

    meta = jnp.stack([piece[:, :, half:] for piece in token_pieces[:2]], axis=1)
    meta = meta.reshape(n_expert, token_count, -1).astype(F32)
    named, high, middle, low = [
        meta[:, :, i * top_count : (i + 1) * top_count] for i in range(4)
    ]
    probs = high + middle + low
    before = (
        jnp.arange(token_count)[:, None] < jnp.arange(token_count)[None, :]
    ).astype(BF)

    def selection(index):
        hit = named == index.astype(F32)
        member = jnp.any(hit, axis=2)
        slot = product(member.astype(BF), before).astype(jnp.int32)
        return hit, jnp.where(member, slot, -1)

    hit, slots = selection(copy)
    _, pair_slots = selection(jnp.bitwise_xor(copy, mine))
    pair_slots = jnp.where(paired[0] == 1, pair_slots, -1)
    select = jnp.arange(capacity, dtype=jnp.int32)[None, :, None] == slots[:, None, :]
    shift = capacity * (jnp.arange(n_expert, dtype=jnp.int32) % 2)[:, None]
    slots, pair_slots = [
        jnp.where(value < 0, value, value + shift) for value in (slots, pair_slots)
    ]
    columns, pair_columns = slots[:, :, None], pair_slots[:, :, None]
    prob = jnp.sum(jnp.where(hit, probs, 0.0), axis=2)
    row_prob = jnp.sum(jnp.where(select, prob[:, None, :], 0.0), axis=2)
    prob_own = lax.dynamic_slice_in_dim(row_prob, dp * mine, mine).reshape(mine * capacity, 1)

    def rows_of(which, pieces, weights, dims, *deps):
        return rows_product(which, slots, pieces, weights, dims, capacity, half, deps)[0]

    def over(value):
        return exchange(value, "dp", 1)

    leaving = rows_of(other_one, token_pieces, [gate_slab, up_slab], NN)
    coming = over(leaving)
    cot_now = join([cot_whole], [cross(cot_whole, 8)], (0, 0), (leaving,), True)
    kept = rows_of(dp_one, token_pieces, [gate_slab, up_slab], NN, cot_now[0])
    cot_now = widen(cot_now, (4, 2), None, (kept,))
    cot_third = [cross(value, bit) for value, bit in zip(cot_now, (2, 4))]
    (hid,) = by_rows(hidden_kernel, [kept, coming, prob_own], 0, 1)
    hid_crossed = cross(hid, mine)
    hid_other = over(hid)
    cot_pieces = finish(widen(cot_now, (2, 4), cot_third, (hid,)))
    leaving = rows_of(other_one, cot_pieces, [down_slab], NT)
    dhid_coming = over(leaving)
    dhid_kept = rows_of(dp_one, cot_pieces, [down_slab], NT)
    out_keep, *out_send = back_product(
        dp_one, columns, [hid, hid_other], [down_slab], NN, capacity, OUT_PARTS, (dhid_kept, leaving)
    )
    (slopes,) = by_rows(
        slopes_kernel,
        [kept, coming, prob_own, dhid_kept, dhid_coming],
        1,
        0,
        (out_send[0], hid_crossed),
    )
    slopes_other = over(slopes)
    slopes_crossed = cross(slopes, mine)

    shape = (2, 2, 2, token_count, slab)

    def first_sum(keep, send, mixed, *deps):
        coming = [cross(value, 1).reshape(shape[:-1] + value.shape[-1:]) for value in send]
        return sum_first(keep.reshape(shape), coming, mixed, deps)

    def next_sum(parts, bits, axis, *deps):
        kept, sent = parts[::2], parts[1::2]
        coming = [cross(value, bit) for value, bit in zip(sent, bits)]
        return sum_split(kept, coming, [axis] * len(kept), axis == 0, deps)

    def end_sum(parts, *deps):
        return last_sum(parts[::2], [cross(value, 8) for value in parts[1::2]], deps)

    def gradient(values, pieces, flat, *deps):
        return weight_gradient(
            dp_one, columns, pair_columns, values, pieces, flat, capacity, half, deps
        )

    out_parts = first_sum(out_keep, out_send, MIXED_OUT)
    out_bits = ((2, 4), (4, 2)) if MIXED_OUT else ((2, 2), (4, 4))
    back_bits = ((2, 4), (4, 2)) if MIXED else ((2, 2), (4, 4))
    back_keep, *back_send = back_product(
        dp_one,
        columns,
        [(slopes, 0), (slopes_other, 0), (slopes, 1), (slopes_other, 1)],
        [gate_slab, up_slab],
        NT,
        capacity,
        BACK_PARTS,
        (out_parts[1],),
    )
    hid_beyond = over(hid_crossed)
    out_parts = next_sum(out_parts, out_bits[0], 1, back_keep)
    back_send[1] = after(back_send[1], out_parts[1])
    back_parts = list(first_sum(back_keep, back_send, MIXED))
    back_parts[3] = after(back_parts[3], slopes_crossed)
    slopes_beyond = [over(slopes_crossed[part]) for part in range(2)]

    def slope_values(part):
        stacks = [(value, part) for value in (slopes, slopes_other, slopes_crossed)]
        return stacks + [slopes_beyond[part]]

    out_parts = next_sum(out_parts, out_bits[1], 0, back_parts[3])
    grad_down = gradient(
        [hid, hid_other, hid_crossed, hid_beyond], cot_pieces, False, back_parts[3]
    )
    output = end_sum(out_parts, grad_down)
    back_parts = next_sum(back_parts, back_bits[0], 1, output)
    grad_gate = gradient(slope_values(0), token_pieces, True, back_parts[1])
    back_parts = next_sum(back_parts, back_bits[1], 0, grad_gate)
    grad_up = gradient(slope_values(1), token_pieces, True, back_parts[1])
    grad_tokens = end_sum(back_parts)
    return (output, grad_tokens, grad_gate[None], grad_up[None], grad_down[None])


def per_device(*arrays):
    quick = lax.axis_size("dp") == 2 and lax.axis_size("expert") == 16
    return (fast if quick else general)(*arrays)


def solution(mesh):
    return jax.shard_map(
        per_device,
        mesh=mesh,
        in_specs=(
            P("expert", "dp"),
            P("expert", None),
            P("expert", None),
            P("expert"),
            P("expert", "dp", None),
            P("expert", "dp", None),
            P("expert", None, "dp"),
            P("expert", "dp"),
        ),
        out_specs=(
            P("expert", "dp"),
            P("expert", "dp"),
            P("expert", "dp", None),
            P("expert", "dp", None),
            P("expert", None, "dp"),
        ),
        check_vma=False,
    )
```

```python
import functools

import jax
import jax.numpy as jnp
from jax import lax
from jax.experimental import pallas as pl
from jax.experimental.pallas import tpu as pltpu
from jax.sharding import PartitionSpec as P

BF = jnp.bfloat16
F32 = jnp.float32


def exchange(value, axis, bit):
    pairs = [(source, source ^ bit) for source in range(lax.axis_size(axis))]
    return lax.ppermute(value, axis, pairs)


def product(left, right):
    return jnp.dot(left, right, preferred_element_type=F32)


def contract(left, right, dims):
    return lax.dot_general(left, right, (dims, ((), ())), preferred_element_type=F32)


def batched(left, right, dims):
    return lax.dot_general(left, right, (dims, ((0,), (0,))), preferred_element_type=F32)


def split_exact(value):
    high = lax.reduce_precision(value, 8, 7)
    rest = value - high
    middle = lax.reduce_precision(rest, 8, 7)
    return [high.astype(BF), middle.astype(BF), (rest - middle).astype(BF)]


def bits_of(count):
    return [1 << place for place in reversed(range(count.bit_length() - 1))]


def gather_sources(block, order, bits, flip):
    current = block.reshape((1,) * len(bits) + block.shape)
    for bit in order:
        place = bits.index(bit)
        other = exchange(current, "expert", bit)
        if flip is not None and place == 0:
            first, second = jnp.where(flip, other, current), jnp.where(flip, current, other)
        else:
            first, second = current, other
        current = jnp.concatenate([first, second], axis=place)
    return current.reshape((2 ** len(bits),) + block.shape)


def scatter_sources(blocks, order, bits, flip):
    current = blocks.reshape((2,) * len(bits) + blocks.shape[1:])
    for bit in order:
        place = bits.index(bit)
        first = lax.slice_in_dim(current, 0, 1, axis=place)
        second = lax.slice_in_dim(current, 1, 2, axis=place)
        if flip is not None and place == 0:
            first, second = jnp.where(flip, second, first), jnp.where(flip, first, second)
        other = exchange(second, "expert", bit)
        current = (first.astype(F32) + other.astype(F32)).astype(BF)
    return current.reshape(blocks.shape[1:])


def general(tokens, routing, gate_probs, paired, w_gate, w_up, w_down, cotangent):
    n_expert = lax.axis_size("expert")
    n_data = lax.axis_size("dp")
    token_count, top_count = routing.shape
    slab = tokens.shape[1]
    hidden = w_gate.shape[2]
    capacity = max(2, 5 * token_count * top_count // (4 * n_expert))
    all_rows = n_expert * capacity
    own_rows = all_rows // n_data
    half = slab // 2
    bits = bits_of(n_expert)
    top = bits[0]
    paired_dp = n_data == 2
    flip = (lax.axis_index("dp") == 1) if paired_dp else None
    copy = lax.axis_index("expert")
    gate_slab, up_slab, down_slab = w_gate[0], w_up[0], w_down[0]
    order_a = list(bits)
    order_b = [bits[0], bits[2], bits[1]] + list(bits[3:])

    meta = jnp.concatenate([routing.astype(BF)] + split_exact(gate_probs), axis=1)
    head = gather_sources(
        jnp.concatenate([tokens[:, :half], meta], axis=1), order_a, bits, flip
    )
    tail = gather_sources(tokens[:, half:], order_b, bits, flip)
    cot_head = gather_sources(cotangent[:, :half], order_a, bits, flip)
    cot_tail = gather_sources(cotangent[:, half:], order_b, bits, flip)

    named = head[:, :, half : half + top_count].astype(F32)
    parts = [
        head[:, :, half + (1 + i) * top_count : half + (2 + i) * top_count].astype(F32)
        for i in range(3)
    ]
    probs = parts[0] + parts[1] + parts[2]
    before = (
        jnp.arange(token_count)[:, None] < jnp.arange(token_count)[None, :]
    ).astype(BF)

    def selection(index):
        hit = named == index.astype(F32)
        member = jnp.any(hit, axis=2)
        slot = product(member.astype(BF), before).astype(jnp.int32)
        slot = jnp.where(member, slot, -1)
        select = jnp.arange(capacity, dtype=jnp.int32)[None, :, None] == slot[:, None, :]
        return select, jnp.sum(jnp.where(hit, probs, 0.0), axis=2)

    select, prob = selection(copy)
    select_pair, _ = selection(copy ^ top)
    row_prob = jnp.sum(jnp.where(select, prob[:, None, :], 0.0), axis=2).reshape(all_rows, 1)
    pick = select.astype(BF)
    keep = paired.astype(F32)[0]
    pick_both = jnp.concatenate(
        [pick, (select_pair.astype(F32) * keep).astype(BF)], axis=1
    )

    def rows_of(blocks):
        return batched(pick, blocks, ((2,), (1,))).astype(BF).reshape(all_rows, -1)

    def to_tokens(chooser, rows):
        rows = rows.reshape(n_expert, -1, rows.shape[-1])
        spread = batched(chooser, rows, ((1,), (1,))).astype(BF)
        return spread.reshape(n_expert * token_count, -1)

    def sum_dp(rows):
        if paired_dp:
            other = exchange(rows[own_rows:], "dp", 1)
            return rows[:own_rows].astype(F32) + other.astype(F32)
        return lax.psum_scatter(rows, "dp", scatter_dimension=0, tiled=True).astype(F32)

    def gather_dp(rows):
        if paired_dp:
            return jnp.concatenate([rows, exchange(rows, "dp", 1)], axis=0)
        return lax.all_gather(rows, "dp", axis=0, tiled=True)

    def gather_pair(rows):
        crossed = exchange(rows, "expert", top)
        if paired_dp:
            return jnp.concatenate([exchange(crossed, "dp", 1), crossed], axis=0)
        everything = lax.all_gather(crossed, "dp", axis=0, tiled=True)
        middle = all_rows // 2
        return jnp.concatenate([everything[middle:], everything[:middle]], axis=0)

    if paired_dp:
        prob_own = row_prob[:own_rows]
    else:
        prob_own = lax.dynamic_slice_in_dim(row_prob, lax.axis_index("dp") * own_rows, own_rows)

    token_all = jnp.concatenate([head[:, :, :half], tail], axis=2)
    cot_all = jnp.concatenate([cot_head, cot_tail], axis=2)
    token_rows = rows_of(token_all)
    gate_up = jnp.concatenate(
        [product(token_rows, gate_slab).astype(BF), product(token_rows, up_slab).astype(BF)],
        axis=1,
    )
    summed = sum_dp(gate_up)
    gate_own, up_own = summed[:, :hidden], summed[:, hidden:]
    cot_rows = rows_of(cot_all)
    grad_hidden = sum_dp(contract(cot_rows, down_slab, ((1,), (1,))).astype(BF)) * prob_own

    sigma = jax.nn.sigmoid(gate_own)
    activated = gate_own * sigma
    hid = (activated * up_own * prob_own).astype(BF)
    grad_rows = jnp.concatenate(
        [
            (grad_hidden * up_own * sigma * (1.0 + gate_own * (1.0 - sigma))).astype(BF),
            (grad_hidden * activated).astype(BF),
        ],
        axis=1,
    )
    hid_all = gather_dp(hid)
    hid_pair = gather_pair(hid)
    grad_all = gather_dp(grad_rows)
    grad_pair = gather_pair(grad_rows)

    out_part = product(to_tokens(pick, hid_all), down_slab).astype(BF)
    output = scatter_halves(out_part, n_expert, bits, flip)
    grad_spread = to_tokens(pick, grad_all)
    back_part = (
        contract(grad_spread[:, :hidden], gate_slab, ((1,), (1,)))
        + contract(grad_spread[:, hidden:], up_slab, ((1,), (1,)))
    ).astype(BF)
    grad_tokens = scatter_halves(back_part, n_expert, bits, flip)

    def both(own, pair):
        return jnp.concatenate(
            [
                own.reshape(n_expert, capacity, -1),
                pair.reshape(n_expert, capacity, -1),
            ],
            axis=1,
        )

    hid_both = to_tokens(pick_both, both(hid_all, hid_pair))
    grad_both = to_tokens(pick_both, both(grad_all, grad_pair))
    token_flat = token_all.reshape(n_expert * token_count, slab)
    cot_flat = cot_all.reshape(n_expert * token_count, slab)
    grad_gate = contract(token_flat, grad_both[:, :hidden], ((0,), (0,)))
    grad_up = contract(token_flat, grad_both[:, hidden:], ((0,), (0,)))
    grad_down = contract(hid_both, cot_flat, ((0,), (0,)))
    return (output, grad_tokens, grad_gate[None], grad_up[None], grad_down[None])


def scatter_halves(part, n_expert, bits, flip):
    half = part.shape[1] // 2
    blocks = part.reshape(n_expert, -1, part.shape[1])
    up = list(reversed(bits))
    first = scatter_sources(blocks[:, :, :half], up, bits, flip)
    other_order = [up[0], up[2], up[1]] + up[3:]
    second = scatter_sources(blocks[:, :, half:], other_order, bits, flip)
    return jnp.concatenate([first, second], axis=1)


VMEM_BYTES = 62 * 2**20
LIGHT = 1000
BACK_TILE = 512
GRAD_TILE = 512
ROWS_TILE = 256
OUT_PARTS = (2, 2, 2, 2)
BACK_PARTS = (3, 3, 2)
CUTS = 1
MIXED = True
MIXED_OUT = True
NN = ((1,), (0,))
NT = ((1,), (1,))
TN = ((0,), (0,))


def call(kernel, grid, in_specs, out_specs, out_shape, scratch, flops, moved, deps=(), prefetch=1):
    held = prefetch + len(in_specs)

    def body(*refs):
        kernel(*refs[:held], *refs[held + len(deps) :])

    run = pl.pallas_call(
        body,
        grid_spec=pltpu.PrefetchScalarGridSpec(
            num_scalar_prefetch=prefetch,
            grid=grid,
            in_specs=in_specs + [pl.BlockSpec(memory_space=pl.ANY)] * len(deps),
            out_specs=out_specs,
            scratch_shapes=scratch,
        ),
        out_shape=out_shape,
        compiler_params=pltpu.CompilerParams(
            dimension_semantics=("arbitrary",) * len(grid), vmem_limit_bytes=VMEM_BYTES
        ),
        cost_estimate=pl.CostEstimate(
            flops=flops // LIGHT, bytes_accessed=moved // LIGHT, transcendentals=0
        ),
    )
    return lambda *operands: run(*operands, *deps)


def whole(value):
    if isinstance(value, tuple):
        stack, part = value
        return pl.BlockSpec((None,) + stack.shape[1:], lambda j, s: (part, 0, 0)), stack
    return fixed(value.shape), value


def fixed(shape):
    return pl.BlockSpec(shape, lambda j, s: (0,) * len(shape))


def rows_kernel(count, dims, capacity, half_ref, slot_ref, *refs):
    pieces = refs[:4]
    weights = refs[4 : 4 + count]
    outs, rows = refs[4 + count : -1], refs[-1]
    width = pieces[0].shape[2]
    tokens = pieces[0].shape[1]

    @pl.when(pl.program_id(0) == 0)
    def _():
        place = lax.broadcasted_iota(jnp.int32, (2 * capacity, 2 * tokens), 0)
        for pair in range(slot_ref.shape[0] // 2):
            slots = [slot_ref[2 * pair + i : 2 * pair + i + 1, :] for i in range(2)]
            pick = (place == jnp.concatenate(slots, axis=1)).astype(F32).astype(BF)
            at = 2 * pair * capacity
            for side in range(2):
                block = jnp.concatenate(
                    [pieces[2 * side + i][pair] for i in range(2)], axis=0
                )
                rows[at : at + 2 * capacity, side * width : (side + 1) * width] = contract(
                    pick, block, NN
                ).astype(BF)

    for w in range(count):
        outs[0][w] = contract(rows[...], weights[w][...], dims).astype(BF)


def rows_product(half, slots, pieces, weights, dims, capacity, width, deps=()):
    sources, tokens = slots.shape
    mine = sources // 2
    depth = mine // 2
    slab = 2 * width
    hidden = weights[0].shape[1] if dims == NN else weights[0].shape[0]
    tile = min(ROWS_TILE, hidden)
    rows = mine * capacity
    weight_spec = (
        pl.BlockSpec((slab, tile), lambda j, s: (0, j))
        if dims == NN
        else pl.BlockSpec((tile, slab), lambda j, s: (j, 0))
    )
    count = len(weights)
    return call(
        functools.partial(rows_kernel, count, dims, capacity),
        (hidden // tile,),
        [pl.BlockSpec((mine, tokens), lambda j, s: (s[0], 0))]
        + [pl.BlockSpec((depth, tokens, width), lambda j, s: (s[0], 0, 0))] * 4
        + [weight_spec] * count,
        [pl.BlockSpec((count, rows, tile), lambda j, s: (0, 0, j))],
        [jax.ShapeDtypeStruct((count, rows, hidden), BF)],
        [pltpu.VMEM((rows, slab), BF)],
        2 * count * rows * slab * hidden,
        2 * slab * (count * hidden + mine * tokens),
        deps,
    )(half, slots, *pieces, *weights)


def spread(dp, column_ref, sources, capacity, act):
    tokens = column_ref.shape[1]
    place = lax.broadcasted_iota(jnp.int32, (2 * tokens, 2 * capacity), 1)
    mine = sources // 2
    for pair in range(mine):
        half, local = divmod(2 * pair, mine)
        upper = jnp.bitwise_xor(dp, half)
        position = local + mine * upper
        column = column_ref[pl.ds(position, 2)].reshape(2 * tokens, 1)
        pick = (place == column).astype(F32).astype(BF)
        start = pl.multiple_of((local // 2 + (mine // 2) * upper) * tokens, tokens)
        act(start, pick, half, local * capacity, position)


def back_kernel(count, dims, capacity, dp_ref, column_ref, *refs):
    values = refs[: 2 * count]
    weights = refs[2 * count : 3 * count]
    spreads = refs[-2 * count :]
    keep_ref, sends = refs[3 * count], refs[3 * count + 1 : -2 * count]
    sources, tokens, _ = column_ref.shape

    @pl.when(pl.program_id(0) == 0)
    def _():
        def act(start, pick, half, at, position):
            for v in range(count):
                rows = values[2 * v + half][at : at + 2 * capacity, :]
                value = contract(pick, rows, NN).astype(BF)
                for parity in range(2):
                    spreads[2 * v + parity][pl.ds(start, tokens), :] = value[
                        parity * tokens : (parity + 1) * tokens
                    ]

        spread(dp_ref[0], column_ref, sources, capacity, act)

    def total(parity):
        value = contract(spreads[parity][...], weights[0][...], dims)
        for v in range(1, count):
            value = value + contract(spreads[2 * v + parity][...], weights[v][...], dims)
        return value.astype(BF)

    keep_ref[...] = total(0)
    sent = total(1)
    tile = sent.shape[1]
    unit = min(256, tile)
    spots = [(send, at) for send in sends for at in range(0, send.shape[1], unit)]
    per = tile // unit
    for step in range(len(spots) // per):

        @pl.when(pl.program_id(0) == step)
        def _():
            for n, (send, at) in enumerate(spots[step * per : (step + 1) * per]):
                send[:, at : at + unit] = sent[:, n * unit : (n + 1) * unit]


def back_product(dp, columns, values, weights, dims, capacity, parts, deps=()):
    sources, tokens, _ = columns.shape
    specs, values = zip(*[whole(value) for value in values])
    hidden = values[0].shape[-1]
    slab = weights[0].shape[1] if dims == NN else weights[0].shape[0]
    tile, unit = BACK_TILE, 256
    count = len(weights)
    out_rows = sources * tokens // 2
    weight_spec = (
        pl.BlockSpec((hidden, tile), lambda j, s: (0, j))
        if dims == NN
        else pl.BlockSpec((tile, hidden), lambda j, s: (j, 0))
    )
    return call(
        functools.partial(back_kernel, count, dims, capacity),
        (slab // tile,),
        [fixed(columns.shape)] + list(specs) + [weight_spec] * count,
        [pl.BlockSpec((out_rows, tile), lambda j, s: (0, j))]
        + [pl.BlockSpec((out_rows, unit * part), lambda j, s: (0, 0)) for part in parts],
        [jax.ShapeDtypeStruct((out_rows, slab), BF)]
        + [jax.ShapeDtypeStruct((out_rows, unit * part), BF) for part in parts],
        [pltpu.VMEM((out_rows, hidden), BF)] * (2 * count),
        4 * count * out_rows * slab * hidden,
        2 * slab * (count * hidden + 2 * out_rows),
        deps,
    )(dp, columns, *values, *weights)


def grad_kernel(flat, capacity, dp_ref, *refs):
    columns, pair_columns = refs[:2]
    own, other, crossed, beyond = refs[2:6]
    pieces = refs[6:10]
    out_ref = refs[10]
    spreads = refs[11:]
    sources, tokens, _ = columns.shape
    mine = sources // 2
    step = pl.program_id(0)

    @pl.when(step == 0)
    def _():
        def act(start, pick, half, at, position):
            place = lax.broadcasted_iota(jnp.int32, (2 * tokens, 2 * capacity), 1)
            column = pair_columns[pl.ds(position, 2)].reshape(2 * tokens, 1)
            pair_pick = (place == column).astype(F32).astype(BF)
            rows = (own, other)[half][at : at + 2 * capacity, :]
            pair_rows = (beyond, crossed)[half][at : at + 2 * capacity, :]
            value = contract(pick, rows, NN) + contract(pair_pick, pair_rows, NN)
            for parity in range(2):
                part = value[parity * tokens : (parity + 1) * tokens]
                if flat:
                    spreads[parity][pl.ds(start, tokens), :] = part.astype(BF)
                else:
                    spreads[parity][:, pl.ds(start, tokens)] = part.T.astype(BF)

        spread(dp_ref[0], columns, sources, capacity, act)

    def product_of(blocks):
        total = None
        for parity in range(2):
            block = blocks[parity][...].reshape(mine * tokens, blocks[parity].shape[2])
            if flat:
                term = contract(block, spreads[parity][...], TN)
            else:
                term = contract(spreads[parity][...], block, NN)
            total = term if total is None else total + term
        out_ref[...] = total

    half_steps = pl.num_programs(0) // 2

    @pl.when(step < half_steps)
    def _():
        product_of(pieces[:2])

    @pl.when(step >= half_steps)
    def _():
        product_of(pieces[2:])


def weight_gradient(dp, columns, pair_columns, values, pieces, flat, capacity, width, deps=()):
    sources, tokens, _ = columns.shape
    specs, values = zip(*[whole(value) for value in values])
    hidden = values[0].shape[-1]
    slab = 2 * width
    tile = min(GRAD_TILE, width)
    steps = slab // tile
    depth = sources // 2
    first = pl.BlockSpec(
        (depth, tokens, tile), lambda j, s: (0, 0, jnp.minimum(j, steps // 2 - 1))
    )
    second = pl.BlockSpec(
        (depth, tokens, tile), lambda j, s: (0, 0, jnp.maximum(j - steps // 2, 0))
    )
    shape = (slab, hidden) if flat else (hidden, slab)
    return call(
        functools.partial(grad_kernel, flat, capacity),
        (steps,),
        [fixed(columns.shape)] * 2 + list(specs) + [first] * 2 + [second] * 2,
        pl.BlockSpec((tile, hidden), lambda j, s: (j, 0))
        if flat
        else pl.BlockSpec((hidden, tile), lambda j, s: (0, j)),
        jax.ShapeDtypeStruct(shape, F32),
        [pltpu.VMEM((depth * tokens, hidden) if flat else (hidden, depth * tokens), BF)] * 2,
        2 * sources * tokens * slab * hidden,
        4 * slab * hidden + 2 * sources * tokens * slab,
        deps,
    )(dp, columns, pair_columns, *values, *pieces)


def split_kernel(axes, merge, *refs):
    count = len(axes)
    for i, axis in enumerate(axes):
        total = refs[2 * i][...] + refs[2 * i + 1][...]
        width = total.shape[-1]
        for side in range(2):
            part = total[(slice(None),) * axis + (side,)]
            if merge:
                refs[2 * count + side][..., i * width : (i + 1) * width] = part
            else:
                refs[2 * count + 2 * i + side][...] = part


def sum_split(kept, coming, axes, merge, deps=()):
    tokens = kept[0].shape[-2]
    chunk = min(64, tokens)
    in_specs, out_specs, out_shape, operands = [], [], [], []
    for k, c, axis in zip(kept, coming, axes):
        lead, width = k.shape[:-2], k.shape[-1]
        spec = pl.BlockSpec(
            lead + (chunk, width), functools.partial(lambda n, j: (0,) * n + (j, 0), len(lead))
        )
        in_specs += [spec, spec]
        operands += [k, c]
        left = lead[:axis] + lead[axis + 1 :]
        width = width * len(kept) if merge else width
        out_specs += [
            pl.BlockSpec(
                left + (chunk, width), functools.partial(lambda n, j: (0,) * n + (j, 0), len(left))
            )
        ] * 2
        out_shape += [jax.ShapeDtypeStruct(left + (tokens, width), BF)] * 2
    return call(
        functools.partial(split_kernel, tuple(axes), merge),
        (tokens // chunk,),
        in_specs,
        out_specs[:2] if merge else out_specs,
        out_shape[:2] if merge else out_shape,
        [],
        0,
        0,
        deps,
        prefetch=0,
    )(*operands)


def first_kernel(mixed, keep, *refs):
    outs, pieces = refs[-4:], refs[:-4]
    each = outs[0].shape[-1]
    at, width = 0, min(256, each)
    for piece in pieces:
        for first in range(0, piece.shape[-1], width):
            total = keep[..., at : at + width] + piece[..., first : first + width]
            right, place = divmod(at, each)
            for side in range(2):
                outs[side + 2 * right][..., place : place + width] = (
                    total[:, side] if mixed and right else total[:, :, side]
                )
            at += width


def sum_first(keep, coming, mixed, deps=()):
    lead, (tokens, width) = keep.shape[:-2], keep.shape[-2:]
    chunk = min(32, tokens)
    four = lambda j: (0, 0, j, 0)
    five = lambda j: (0, 0, 0, j, 0)
    outs = 4
    each = 2 * width // outs
    return call(
        functools.partial(first_kernel, mixed),
        (tokens // chunk,),
        [pl.BlockSpec(lead + (chunk, value.shape[-1]), five) for value in [keep] + coming],
        [pl.BlockSpec(lead[:2] + (chunk, each), four)] * outs,
        [jax.ShapeDtypeStruct(lead[:2] + (tokens, each), BF)] * outs,
        [],
        0,
        0,
        deps,
        prefetch=0,
    )(keep, *coming)


def last_kernel(*refs):
    width = refs[0].shape[1]
    for i in range(len(refs) // 2):
        refs[-1][:, i * width : (i + 1) * width] = refs[2 * i][...] + refs[2 * i + 1][...]


def last_sum(kept, coming, deps=()):
    tokens, width = kept[0].shape
    spec = pl.BlockSpec((tokens, width), lambda j: (0, 0))
    count = len(kept)
    return call(
        last_kernel,
        (1,),
        [spec] * (2 * count),
        pl.BlockSpec((tokens, count * width), lambda j: (0, 0)),
        jax.ShapeDtypeStruct((tokens, count * width), BF),
        [],
        0,
        0,
        deps,
        prefetch=0,
    )(*[value for pair in zip(kept, coming) for value in pair])


def join_kernel(axes, cut, *refs):
    count = len(axes)
    held = 2 if cut else 2 * count
    outs, stages = refs[held : held + count], refs[held + count : held + 2 * count]
    in_sems, out_sems = refs[held + 2 * count :]
    reads, writes = [], []
    for i, axis in enumerate(axes):
        width = outs[i].shape[-1]
        for side in range(2):
            n = 2 * i + side
            at = (slice(None),) * axis + (slice(side, side + 1),)
            source = refs[side].at[..., i * width : (i + 1) * width] if cut else refs[n]
            reads.append(pltpu.make_async_copy(source, stages[i].at[at], in_sems.at[n]))
            writes.append(
                pltpu.make_async_copy(stages[i].at[at], outs[i].at[at], out_sems.at[n])
            )
    for copy in reads:
        copy.start()
    for read, write in zip(reads, writes):
        read.wait()
        write.start()
    for copy in writes:
        copy.wait()


def join(now, coming, axes, deps=(), cut=False):
    out_shape, operands = [], []
    for value, other in zip(now, coming):
        operands += [value, other]
    for i, axis in enumerate(axes):
        value = now[0 if cut else i]
        shape = value.shape[:axis] + (2,) + value.shape[axis + 1 : -1]
        width = value.shape[-1] // (2 if cut else 1)
        out_shape.append(jax.ShapeDtypeStruct(shape + (width,), BF))
    place = pl.BlockSpec(memory_space=pl.ANY)
    return call(
        functools.partial(join_kernel, tuple(axes), cut),
        (),
        [place] * len(operands),
        [place] * len(out_shape),
        out_shape,
        [pltpu.VMEM(whole.shape, BF) for whole in out_shape]
        + [pltpu.SemaphoreType.DMA((2 * len(axes),))] * 2,
        0,
        0,
        deps,
        prefetch=0,
    )(*operands)


def hidden_kernel(kept, coming, prob, out):
    gate = kept[0].astype(F32) + coming[0].astype(F32)
    up = kept[1].astype(F32) + coming[1].astype(F32)
    out[...] = (gate * jax.nn.sigmoid(gate) * up * prob[...]).astype(BF)


def slopes_kernel(kept, coming, prob, grad_kept, grad_coming, out):
    gate = kept[0].astype(F32) + coming[0].astype(F32)
    up = kept[1].astype(F32) + coming[1].astype(F32)
    grad = (grad_kept[0].astype(F32) + grad_coming[0].astype(F32)) * prob[...]
    sigma = jax.nn.sigmoid(gate)
    out[0] = (grad * up * sigma * (1.0 + gate * (1.0 - sigma))).astype(BF)
    out[1] = (grad * gate * sigma).astype(BF)


def by_rows(kernel, operands, stacks, outs, deps=()):
    rows, hidden = operands[0].shape[1:]
    chunk = rows // 2 if rows % 32 == 0 else rows
    return call(
        kernel,
        (rows // chunk,),
        [
            pl.BlockSpec((chunk, 1), lambda j: (j, 0))
            if value.ndim == 2
            else pl.BlockSpec((value.shape[0], chunk, hidden), lambda j: (0, j, 0))
            for value in operands
        ],
        [pl.BlockSpec((2, chunk, hidden), lambda j: (0, j, 0))] * stacks
        + [pl.BlockSpec((chunk, hidden), lambda j: (j, 0))] * outs,
        [jax.ShapeDtypeStruct((2, rows, hidden), BF)] * stacks
        + [jax.ShapeDtypeStruct((rows, hidden), BF)] * outs,
        [],
        0,
        0,
        deps,
        prefetch=0,
    )(*operands)


def nothing_kernel(*refs):
    pass


def after(value, *others):
    return pl.pallas_call(
        nothing_kernel,
        in_specs=[pl.BlockSpec(memory_space=pl.ANY)] * (1 + len(others)),
        out_specs=pl.BlockSpec(memory_space=pl.ANY),
        out_shape=jax.ShapeDtypeStruct(value.shape, value.dtype),
        input_output_aliases={0: 0},
    )(value, *others)


def fast(tokens, routing, gate_probs, paired, w_gate, w_up, w_down, cotangent):
    n_expert = lax.axis_size("expert")
    token_count, top_count = routing.shape
    slab = tokens.shape[1]
    hidden = w_gate.shape[2]
    capacity = max(2, 5 * token_count * top_count // (4 * n_expert))
    half = slab // 2
    mine = n_expert // 2
    copy = lax.axis_index("expert")
    dp = lax.axis_index("dp").astype(jnp.int32)
    dp_one = dp.reshape(1)
    other_one = (1 - dp).reshape(1)
    gate_slab, up_slab, down_slab = w_gate[0], w_up[0], w_down[0]

    def cross(value, bit):
        return exchange(value, "expert", bit)

    meta = jnp.concatenate([routing.astype(BF)] + split_exact(gate_probs), axis=1)
    meta = jnp.pad(meta, ((0, 0), (0, 128 - meta.shape[1])))

    def blocks(value):
        return [value[:, :half].reshape(1, 1, 1, token_count, half), value[:, half:].reshape(1, 1, 1, token_count, half)]

    def widen(now, bits, coming=None, deps=()):
        if coming is None:
            coming = [cross(value, bit) for value, bit in zip(now, bits)]
        axis = {8: 0, 4: 1, 2: 2}
        return join(now, coming, [axis[bit] for bit in bits], deps)

    token_now = blocks(tokens)
    token_now[0] = jnp.concatenate([token_now[0], meta.reshape(1, 1, 1, token_count, -1)], axis=-1)
    token_now = widen(token_now, (8, 8))
    token_now = widen(token_now, (4, 2))
    token_now = widen(token_now, (2, 4))
    cot_whole = cotangent.reshape(1, 1, 1, token_count, slab)

    def finish(now):
        pieces = []
        for value in now:
            value = value.reshape(mine, token_count, -1)
            pieces += [value, cross(value, 1)]
        return pieces

    token_pieces = finish(token_now)

    meta = jnp.stack([piece[:, :, half:] for piece in token_pieces[:2]], axis=1)
    meta = meta.reshape(n_expert, token_count, -1).astype(F32)
    named, high, middle, low = [
        meta[:, :, i * top_count : (i + 1) * top_count] for i in range(4)
    ]
    probs = high + middle + low
    before = (
        jnp.arange(token_count)[:, None] < jnp.arange(token_count)[None, :]
    ).astype(BF)

    def selection(index):
        hit = named == index.astype(F32)
        member = jnp.any(hit, axis=2)
        slot = product(member.astype(BF), before).astype(jnp.int32)
        return hit, jnp.where(member, slot, -1)

    hit, slots = selection(copy)
    _, pair_slots = selection(jnp.bitwise_xor(copy, mine))
    pair_slots = jnp.where(paired[0] == 1, pair_slots, -1)
    select = jnp.arange(capacity, dtype=jnp.int32)[None, :, None] == slots[:, None, :]
    shift = capacity * (jnp.arange(n_expert, dtype=jnp.int32) % 2)[:, None]
    slots, pair_slots = [
        jnp.where(value < 0, value, value + shift) for value in (slots, pair_slots)
    ]
    columns, pair_columns = slots[:, :, None], pair_slots[:, :, None]
    prob = jnp.sum(jnp.where(hit, probs, 0.0), axis=2)
    row_prob = jnp.sum(jnp.where(select, prob[:, None, :], 0.0), axis=2)
    prob_own = lax.dynamic_slice_in_dim(row_prob, dp * mine, mine).reshape(mine * capacity, 1)

    def rows_of(which, pieces, weights, dims, *deps):
        return rows_product(which, slots, pieces, weights, dims, capacity, half, deps)[0]

    def over(value):
        return exchange(value, "dp", 1)

    leaving = rows_of(other_one, token_pieces, [gate_slab, up_slab], NN)
    coming = over(leaving)
    cot_now = join([cot_whole], [cross(cot_whole, 8)], (0, 0), (leaving,), True)
    kept = rows_of(dp_one, token_pieces, [gate_slab, up_slab], NN, cot_now[0])
    cot_now = widen(cot_now, (4, 2), None, (kept,))
    cot_third = [cross(value, bit) for value, bit in zip(cot_now, (2, 4))]
    (hid,) = by_rows(hidden_kernel, [kept, coming, prob_own], 0, 1)
    hid_crossed = cross(hid, mine)
    hid_other = over(hid)
    cot_pieces = finish(widen(cot_now, (2, 4), cot_third, (hid,)))
    leaving = rows_of(other_one, cot_pieces, [down_slab], NT)
    dhid_coming = over(leaving)
    dhid_kept = rows_of(dp_one, cot_pieces, [down_slab], NT)
    out_keep, *out_send = back_product(
        dp_one, columns, [hid, hid_other], [down_slab], NN, capacity, OUT_PARTS, (dhid_kept, leaving)
    )
    (slopes,) = by_rows(
        slopes_kernel,
        [kept, coming, prob_own, dhid_kept, dhid_coming],
        1,
        0,
        (out_send[0], hid_crossed),
    )
    slopes_other = over(slopes)
    slopes_crossed = cross(slopes, mine)

    shape = (2, 2, 2, token_count, slab)

    def first_sum(keep, send, mixed, *deps):
        coming = [cross(value, 1).reshape(shape[:-1] + value.shape[-1:]) for value in send]
        return sum_first(keep.reshape(shape), coming, mixed, deps)

    def next_sum(parts, bits, axis, *deps):
        kept, sent = parts[::2], parts[1::2]
        coming = [cross(value, bit) for value, bit in zip(sent, bits)]
        return sum_split(kept, coming, [axis] * len(kept), axis == 0, deps)

    def end_sum(parts, *deps):
        return last_sum(parts[::2], [cross(value, 8) for value in parts[1::2]], deps)

    def gradient(values, pieces, flat, *deps):
        return weight_gradient(
            dp_one, columns, pair_columns, values, pieces, flat, capacity, half, deps
        )

    out_parts = first_sum(out_keep, out_send, MIXED_OUT)
    out_bits = ((2, 4), (4, 2)) if MIXED_OUT else ((2, 2), (4, 4))
    back_bits = ((2, 4), (4, 2)) if MIXED else ((2, 2), (4, 4))
    back_keep, *back_send = back_product(
        dp_one,
        columns,
        [(slopes, 0), (slopes_other, 0), (slopes, 1), (slopes_other, 1)],
        [gate_slab, up_slab],
        NT,
        capacity,
        BACK_PARTS,
        (out_parts[1],),
    )
    hid_beyond = over(hid_crossed)
    out_parts = next_sum(out_parts, out_bits[0], 1, back_keep)
    back_send[1] = after(back_send[1], out_parts[1])
    back_parts = list(first_sum(back_keep, back_send, MIXED))
    back_parts[3] = after(back_parts[3], slopes_crossed, hid_beyond)
    slopes_beyond = [over(slopes_crossed[part]) for part in range(2)]

    def slope_values(part):
        stacks = [(value, part) for value in (slopes, slopes_other, slopes_crossed)]
        return stacks + [slopes_beyond[part]]

    out_parts = next_sum(out_parts, out_bits[1], 0, back_parts[3])
    grad_down = gradient(
        [hid, hid_other, hid_crossed, hid_beyond], cot_pieces, False, out_parts[1]
    )
    output = end_sum(out_parts, grad_down)
    back_parts = next_sum(back_parts, back_bits[0], 1, output)
    grad_gate = gradient(slope_values(0), token_pieces, True, back_parts[1])
    back_parts = next_sum(back_parts, back_bits[1], 0, grad_gate)
    grad_up = gradient(slope_values(1), token_pieces, True, back_parts[1])
    grad_tokens = end_sum(back_parts)
    return (output, grad_tokens, grad_gate[None], grad_up[None], grad_down[None])


def per_device(*arrays):
    quick = lax.axis_size("dp") == 2 and lax.axis_size("expert") == 16
    return (fast if quick else general)(*arrays)


def solution(mesh):
    return jax.shard_map(
        per_device,
        mesh=mesh,
        in_specs=(
            P("expert", "dp"),
            P("expert", None),
            P("expert", None),
            P("expert"),
            P("expert", "dp", None),
            P("expert", "dp", None),
            P("expert", None, "dp"),
            P("expert", "dp"),
        ),
        out_specs=(
            P("expert", "dp"),
            P("expert", "dp"),
            P("expert", "dp", None),
            P("expert", "dp", None),
            P("expert", None, "dp"),
        ),
        check_vma=False,
    )
```

```python
import functools

import jax
import jax.numpy as jnp
from jax import lax
from jax.experimental import pallas as pl
from jax.experimental.pallas import tpu as pltpu
from jax.sharding import PartitionSpec as P

BF = jnp.bfloat16
F32 = jnp.float32


def exchange(value, axis, bit):
    pairs = [(source, source ^ bit) for source in range(lax.axis_size(axis))]
    return lax.ppermute(value, axis, pairs)


def product(left, right):
    return jnp.dot(left, right, preferred_element_type=F32)


def contract(left, right, dims):
    return lax.dot_general(left, right, (dims, ((), ())), preferred_element_type=F32)


def batched(left, right, dims):
    return lax.dot_general(left, right, (dims, ((0,), (0,))), preferred_element_type=F32)


def split_exact(value):
    high = lax.reduce_precision(value, 8, 7)
    rest = value - high
    middle = lax.reduce_precision(rest, 8, 7)
    return [high.astype(BF), middle.astype(BF), (rest - middle).astype(BF)]


def bits_of(count):
    return [1 << place for place in reversed(range(count.bit_length() - 1))]


def gather_sources(block, order, bits, flip):
    current = block.reshape((1,) * len(bits) + block.shape)
    for bit in order:
        place = bits.index(bit)
        other = exchange(current, "expert", bit)
        if flip is not None and place == 0:
            first, second = jnp.where(flip, other, current), jnp.where(flip, current, other)
        else:
            first, second = current, other
        current = jnp.concatenate([first, second], axis=place)
    return current.reshape((2 ** len(bits),) + block.shape)


def scatter_sources(blocks, order, bits, flip):
    current = blocks.reshape((2,) * len(bits) + blocks.shape[1:])
    for bit in order:
        place = bits.index(bit)
        first = lax.slice_in_dim(current, 0, 1, axis=place)
        second = lax.slice_in_dim(current, 1, 2, axis=place)
        if flip is not None and place == 0:
            first, second = jnp.where(flip, second, first), jnp.where(flip, first, second)
        other = exchange(second, "expert", bit)
        current = (first.astype(F32) + other.astype(F32)).astype(BF)
    return current.reshape(blocks.shape[1:])


def general(tokens, routing, gate_probs, paired, w_gate, w_up, w_down, cotangent):
    n_expert = lax.axis_size("expert")
    n_data = lax.axis_size("dp")
    token_count, top_count = routing.shape
    slab = tokens.shape[1]
    hidden = w_gate.shape[2]
    capacity = max(2, 5 * token_count * top_count // (4 * n_expert))
    all_rows = n_expert * capacity
    own_rows = all_rows // n_data
    half = slab // 2
    bits = bits_of(n_expert)
    top = bits[0]
    paired_dp = n_data == 2
    flip = (lax.axis_index("dp") == 1) if paired_dp else None
    copy = lax.axis_index("expert")
    gate_slab, up_slab, down_slab = w_gate[0], w_up[0], w_down[0]
    order_a = list(bits)
    order_b = [bits[0], bits[2], bits[1]] + list(bits[3:])

    meta = jnp.concatenate([routing.astype(BF)] + split_exact(gate_probs), axis=1)
    head = gather_sources(
        jnp.concatenate([tokens[:, :half], meta], axis=1), order_a, bits, flip
    )
    tail = gather_sources(tokens[:, half:], order_b, bits, flip)
    cot_head = gather_sources(cotangent[:, :half], order_a, bits, flip)
    cot_tail = gather_sources(cotangent[:, half:], order_b, bits, flip)

    named = head[:, :, half : half + top_count].astype(F32)
    parts = [
        head[:, :, half + (1 + i) * top_count : half + (2 + i) * top_count].astype(F32)
        for i in range(3)
    ]
    probs = parts[0] + parts[1] + parts[2]
    before = (
        jnp.arange(token_count)[:, None] < jnp.arange(token_count)[None, :]
    ).astype(BF)

    def selection(index):
        hit = named == index.astype(F32)
        member = jnp.any(hit, axis=2)
        slot = product(member.astype(BF), before).astype(jnp.int32)
        slot = jnp.where(member, slot, -1)
        select = jnp.arange(capacity, dtype=jnp.int32)[None, :, None] == slot[:, None, :]
        return select, jnp.sum(jnp.where(hit, probs, 0.0), axis=2)

    select, prob = selection(copy)
    select_pair, _ = selection(copy ^ top)
    row_prob = jnp.sum(jnp.where(select, prob[:, None, :], 0.0), axis=2).reshape(all_rows, 1)
    pick = select.astype(BF)
    keep = paired.astype(F32)[0]
    pick_both = jnp.concatenate(
        [pick, (select_pair.astype(F32) * keep).astype(BF)], axis=1
    )

    def rows_of(blocks):
        return batched(pick, blocks, ((2,), (1,))).astype(BF).reshape(all_rows, -1)

    def to_tokens(chooser, rows):
        rows = rows.reshape(n_expert, -1, rows.shape[-1])
        spread = batched(chooser, rows, ((1,), (1,))).astype(BF)
        return spread.reshape(n_expert * token_count, -1)

    def sum_dp(rows):
        if paired_dp:
            other = exchange(rows[own_rows:], "dp", 1)
            return rows[:own_rows].astype(F32) + other.astype(F32)
        return lax.psum_scatter(rows, "dp", scatter_dimension=0, tiled=True).astype(F32)

    def gather_dp(rows):
        if paired_dp:
            return jnp.concatenate([rows, exchange(rows, "dp", 1)], axis=0)
        return lax.all_gather(rows, "dp", axis=0, tiled=True)

    def gather_pair(rows):
        crossed = exchange(rows, "expert", top)
        if paired_dp:
            return jnp.concatenate([exchange(crossed, "dp", 1), crossed], axis=0)
        everything = lax.all_gather(crossed, "dp", axis=0, tiled=True)
        middle = all_rows // 2
        return jnp.concatenate([everything[middle:], everything[:middle]], axis=0)

    if paired_dp:
        prob_own = row_prob[:own_rows]
    else:
        prob_own = lax.dynamic_slice_in_dim(row_prob, lax.axis_index("dp") * own_rows, own_rows)

    token_all = jnp.concatenate([head[:, :, :half], tail], axis=2)
    cot_all = jnp.concatenate([cot_head, cot_tail], axis=2)
    token_rows = rows_of(token_all)
    gate_up = jnp.concatenate(
        [product(token_rows, gate_slab).astype(BF), product(token_rows, up_slab).astype(BF)],
        axis=1,
    )
    summed = sum_dp(gate_up)
    gate_own, up_own = summed[:, :hidden], summed[:, hidden:]
    cot_rows = rows_of(cot_all)
    grad_hidden = sum_dp(contract(cot_rows, down_slab, ((1,), (1,))).astype(BF)) * prob_own

    sigma = jax.nn.sigmoid(gate_own)
    activated = gate_own * sigma
    hid = (activated * up_own * prob_own).astype(BF)
    grad_rows = jnp.concatenate(
        [
            (grad_hidden * up_own * sigma * (1.0 + gate_own * (1.0 - sigma))).astype(BF),
            (grad_hidden * activated).astype(BF),
        ],
        axis=1,
    )
    hid_all = gather_dp(hid)
    hid_pair = gather_pair(hid)
    grad_all = gather_dp(grad_rows)
    grad_pair = gather_pair(grad_rows)

    out_part = product(to_tokens(pick, hid_all), down_slab).astype(BF)
    output = scatter_halves(out_part, n_expert, bits, flip)
    grad_spread = to_tokens(pick, grad_all)
    back_part = (
        contract(grad_spread[:, :hidden], gate_slab, ((1,), (1,)))
        + contract(grad_spread[:, hidden:], up_slab, ((1,), (1,)))
    ).astype(BF)
    grad_tokens = scatter_halves(back_part, n_expert, bits, flip)

    def both(own, pair):
        return jnp.concatenate(
            [
                own.reshape(n_expert, capacity, -1),
                pair.reshape(n_expert, capacity, -1),
            ],
            axis=1,
        )

    hid_both = to_tokens(pick_both, both(hid_all, hid_pair))
    grad_both = to_tokens(pick_both, both(grad_all, grad_pair))
    token_flat = token_all.reshape(n_expert * token_count, slab)
    cot_flat = cot_all.reshape(n_expert * token_count, slab)
    grad_gate = contract(token_flat, grad_both[:, :hidden], ((0,), (0,)))
    grad_up = contract(token_flat, grad_both[:, hidden:], ((0,), (0,)))
    grad_down = contract(hid_both, cot_flat, ((0,), (0,)))
    return (output, grad_tokens, grad_gate[None], grad_up[None], grad_down[None])


def scatter_halves(part, n_expert, bits, flip):
    half = part.shape[1] // 2
    blocks = part.reshape(n_expert, -1, part.shape[1])
    up = list(reversed(bits))
    first = scatter_sources(blocks[:, :, :half], up, bits, flip)
    other_order = [up[0], up[2], up[1]] + up[3:]
    second = scatter_sources(blocks[:, :, half:], other_order, bits, flip)
    return jnp.concatenate([first, second], axis=1)


VMEM_BYTES = 48 * 2**20
LIGHT = 1000
BACK_TILE = 512
GRAD_TILE = 512
ROWS_TILE = 256
OUT_PARTS = (2, 2, 2, 2)
BACK_PARTS = (3, 3, 2)
CUTS = 1
MIXED = True
MIXED_OUT = True
NN = ((1,), (0,))
NT = ((1,), (1,))
TN = ((0,), (0,))


def call(kernel, grid, in_specs, out_specs, out_shape, scratch, flops, moved, deps=(), prefetch=1):
    held = prefetch + len(in_specs)

    def body(*refs):
        kernel(*refs[:held], *refs[held + len(deps) :])

    run = pl.pallas_call(
        body,
        grid_spec=pltpu.PrefetchScalarGridSpec(
            num_scalar_prefetch=prefetch,
            grid=grid,
            in_specs=in_specs + [pl.BlockSpec(memory_space=pl.ANY)] * len(deps),
            out_specs=out_specs,
            scratch_shapes=scratch,
        ),
        out_shape=out_shape,
        compiler_params=pltpu.CompilerParams(
            dimension_semantics=("arbitrary",) * len(grid), vmem_limit_bytes=VMEM_BYTES
        ),
        cost_estimate=pl.CostEstimate(
            flops=flops // LIGHT, bytes_accessed=moved // LIGHT, transcendentals=0
        ),
    )
    return lambda *operands: run(*operands, *deps)


def whole(value):
    if isinstance(value, tuple):
        stack, part = value
        return pl.BlockSpec((None,) + stack.shape[1:], lambda j, s: (part, 0, 0)), stack
    return fixed(value.shape), value


def fixed(shape):
    return pl.BlockSpec(shape, lambda j, s: (0,) * len(shape))


def rows_kernel(count, dims, capacity, half_ref, slot_ref, *refs):
    pieces = refs[:4]
    weights = refs[4 : 4 + count]
    outs, rows = refs[4 + count : -1], refs[-1]
    width = pieces[0].shape[2]
    tokens = pieces[0].shape[1]

    @pl.when(pl.program_id(0) == 0)
    def _():
        place = lax.broadcasted_iota(jnp.int32, (2 * capacity, 2 * tokens), 0)
        for pair in range(slot_ref.shape[0] // 2):
            slots = [slot_ref[2 * pair + i : 2 * pair + i + 1, :] for i in range(2)]
            pick = (place == jnp.concatenate(slots, axis=1)).astype(F32).astype(BF)
            at = 2 * pair * capacity
            for side in range(2):
                block = jnp.concatenate(
                    [pieces[2 * side + i][pair] for i in range(2)], axis=0
                )
                rows[at : at + 2 * capacity, side * width : (side + 1) * width] = contract(
                    pick, block, NN
                ).astype(BF)

    for w in range(count):
        outs[0][w] = contract(rows[...], weights[w][...], dims).astype(BF)


def rows_product(half, slots, pieces, weights, dims, capacity, width, deps=()):
    sources, tokens = slots.shape
    mine = sources // 2
    depth = mine // 2
    slab = 2 * width
    hidden = weights[0].shape[1] if dims == NN else weights[0].shape[0]
    tile = min(ROWS_TILE, hidden)
    rows = mine * capacity
    weight_spec = (
        pl.BlockSpec((slab, tile), lambda j, s: (0, j))
        if dims == NN
        else pl.BlockSpec((tile, slab), lambda j, s: (j, 0))
    )
    count = len(weights)
    return call(
        functools.partial(rows_kernel, count, dims, capacity),
        (hidden // tile,),
        [pl.BlockSpec((mine, tokens), lambda j, s: (s[0], 0))]
        + [pl.BlockSpec((depth, tokens, width), lambda j, s: (s[0], 0, 0))] * 4
        + [weight_spec] * count,
        [pl.BlockSpec((count, rows, tile), lambda j, s: (0, 0, j))],
        [jax.ShapeDtypeStruct((count, rows, hidden), BF)],
        [pltpu.VMEM((rows, slab), BF)],
        2 * count * rows * slab * hidden,
        2 * slab * (count * hidden + mine * tokens),
        deps,
    )(half, slots, *pieces, *weights)


def spread(dp, column_ref, sources, capacity, act):
    tokens = column_ref.shape[1]
    place = lax.broadcasted_iota(jnp.int32, (2 * tokens, 2 * capacity), 1)
    mine = sources // 2
    for pair in range(mine):
        half, local = divmod(2 * pair, mine)
        upper = jnp.bitwise_xor(dp, half)
        position = local + mine * upper
        column = column_ref[pl.ds(position, 2)].reshape(2 * tokens, 1)
        pick = (place == column).astype(F32).astype(BF)
        start = pl.multiple_of((local // 2 + (mine // 2) * upper) * tokens, tokens)
        act(start, pick, half, local * capacity, position)


def back_kernel(count, dims, capacity, dp_ref, column_ref, *refs):
    values = refs[: 2 * count]
    weights = refs[2 * count : 3 * count]
    spreads = refs[-2 * count :]
    keep_ref, sends = refs[3 * count], refs[3 * count + 1 : -2 * count]
    sources, tokens, _ = column_ref.shape

    @pl.when(pl.program_id(0) == 0)
    def _():
        def act(start, pick, half, at, position):
            for v in range(count):
                rows = values[2 * v + half][at : at + 2 * capacity, :]
                value = contract(pick, rows, NN).astype(BF)
                for parity in range(2):
                    spreads[2 * v + parity][pl.ds(start, tokens), :] = value[
                        parity * tokens : (parity + 1) * tokens
                    ]

        spread(dp_ref[0], column_ref, sources, capacity, act)

    def total(parity):
        value = contract(spreads[parity][...], weights[0][...], dims)
        for v in range(1, count):
            value = value + contract(spreads[2 * v + parity][...], weights[v][...], dims)
        return value.astype(BF)

    keep_ref[...] = total(0)
    sent = total(1)
    tile = sent.shape[1]
    unit = min(256, tile)
    spots = [(send, at) for send in sends for at in range(0, send.shape[1], unit)]
    per = tile // unit
    for step in range(len(spots) // per):

        @pl.when(pl.program_id(0) == step)
        def _():
            for n, (send, at) in enumerate(spots[step * per : (step + 1) * per]):
                send[:, at : at + unit] = sent[:, n * unit : (n + 1) * unit]


def back_product(dp, columns, values, weights, dims, capacity, parts, deps=()):
    sources, tokens, _ = columns.shape
    specs, values = zip(*[whole(value) for value in values])
    hidden = values[0].shape[-1]
    slab = weights[0].shape[1] if dims == NN else weights[0].shape[0]
    tile, unit = BACK_TILE, 256
    count = len(weights)
    out_rows = sources * tokens // 2
    weight_spec = (
        pl.BlockSpec((hidden, tile), lambda j, s: (0, j))
        if dims == NN
        else pl.BlockSpec((tile, hidden), lambda j, s: (j, 0))
    )
    return call(
        functools.partial(back_kernel, count, dims, capacity),
        (slab // tile,),
        [fixed(columns.shape)] + list(specs) + [weight_spec] * count,
        [pl.BlockSpec((out_rows, tile), lambda j, s: (0, j))]
        + [pl.BlockSpec((out_rows, unit * part), lambda j, s: (0, 0)) for part in parts],
        [jax.ShapeDtypeStruct((out_rows, slab), BF)]
        + [jax.ShapeDtypeStruct((out_rows, unit * part), BF) for part in parts],
        [pltpu.VMEM((out_rows, hidden), BF)] * (2 * count),
        4 * count * out_rows * slab * hidden,
        2 * slab * (count * hidden + 2 * out_rows),
        deps,
    )(dp, columns, *values, *weights)


def grad_kernel(flat, capacity, dp_ref, *refs):
    columns, pair_columns = refs[:2]
    own, other, crossed, beyond = refs[2:6]
    pieces = refs[6:10]
    out_ref = refs[10]
    spreads = refs[11:]
    sources, tokens, _ = columns.shape
    mine = sources // 2
    step = pl.program_id(0)

    @pl.when(step == 0)
    def _():
        def act(start, pick, half, at, position):
            place = lax.broadcasted_iota(jnp.int32, (2 * tokens, 2 * capacity), 1)
            column = pair_columns[pl.ds(position, 2)].reshape(2 * tokens, 1)
            pair_pick = (place == column).astype(F32).astype(BF)
            rows = (own, other)[half][at : at + 2 * capacity, :]
            pair_rows = (beyond, crossed)[half][at : at + 2 * capacity, :]
            value = contract(pick, rows, NN) + contract(pair_pick, pair_rows, NN)
            for parity in range(2):
                part = value[parity * tokens : (parity + 1) * tokens]
                if flat:
                    spreads[parity][pl.ds(start, tokens), :] = part.astype(BF)
                else:
                    spreads[parity][:, pl.ds(start, tokens)] = part.T.astype(BF)

        spread(dp_ref[0], columns, sources, capacity, act)

    def product_of(blocks):
        total = None
        for parity in range(2):
            block = blocks[parity][...].reshape(mine * tokens, blocks[parity].shape[2])
            if flat:
                term = contract(block, spreads[parity][...], TN)
            else:
                term = contract(spreads[parity][...], block, NN)
            total = term if total is None else total + term
        out_ref[...] = total

    half_steps = pl.num_programs(0) // 2

    @pl.when(step < half_steps)
    def _():
        product_of(pieces[:2])

    @pl.when(step >= half_steps)
    def _():
        product_of(pieces[2:])


def weight_gradient(dp, columns, pair_columns, values, pieces, flat, capacity, width, deps=()):
    sources, tokens, _ = columns.shape
    specs, values = zip(*[whole(value) for value in values])
    hidden = values[0].shape[-1]
    slab = 2 * width
    tile = min(GRAD_TILE, width)
    steps = slab // tile
    depth = sources // 2
    first = pl.BlockSpec(
        (depth, tokens, tile), lambda j, s: (0, 0, jnp.minimum(j, steps // 2 - 1))
    )
    second = pl.BlockSpec(
        (depth, tokens, tile), lambda j, s: (0, 0, jnp.maximum(j - steps // 2, 0))
    )
    shape = (slab, hidden) if flat else (hidden, slab)
    return call(
        functools.partial(grad_kernel, flat, capacity),
        (steps,),
        [fixed(columns.shape)] * 2 + list(specs) + [first] * 2 + [second] * 2,
        pl.BlockSpec((tile, hidden), lambda j, s: (j, 0))
        if flat
        else pl.BlockSpec((hidden, tile), lambda j, s: (0, j)),
        jax.ShapeDtypeStruct(shape, F32),
        [pltpu.VMEM((depth * tokens, hidden) if flat else (hidden, depth * tokens), BF)] * 2,
        2 * sources * tokens * slab * hidden,
        4 * slab * hidden + 2 * sources * tokens * slab,
        deps,
    )(dp, columns, pair_columns, *values, *pieces)


def split_kernel(axes, merge, *refs):
    count = len(axes)
    for i, axis in enumerate(axes):
        total = refs[2 * i][...] + refs[2 * i + 1][...]
        width = total.shape[-1]
        for side in range(2):
            part = total[(slice(None),) * axis + (side,)]
            if merge:
                refs[2 * count + side][..., i * width : (i + 1) * width] = part
            else:
                refs[2 * count + 2 * i + side][...] = part


def sum_split(kept, coming, axes, merge, deps=()):
    tokens = kept[0].shape[-2]
    chunk = min(64, tokens)
    in_specs, out_specs, out_shape, operands = [], [], [], []
    for k, c, axis in zip(kept, coming, axes):
        lead, width = k.shape[:-2], k.shape[-1]
        spec = pl.BlockSpec(
            lead + (chunk, width), functools.partial(lambda n, j: (0,) * n + (j, 0), len(lead))
        )
        in_specs += [spec, spec]
        operands += [k, c]
        left = lead[:axis] + lead[axis + 1 :]
        width = width * len(kept) if merge else width
        out_specs += [
            pl.BlockSpec(
                left + (chunk, width), functools.partial(lambda n, j: (0,) * n + (j, 0), len(left))
            )
        ] * 2
        out_shape += [jax.ShapeDtypeStruct(left + (tokens, width), BF)] * 2
    return call(
        functools.partial(split_kernel, tuple(axes), merge),
        (tokens // chunk,),
        in_specs,
        out_specs[:2] if merge else out_specs,
        out_shape[:2] if merge else out_shape,
        [],
        0,
        0,
        deps,
        prefetch=0,
    )(*operands)


def first_kernel(mixed, keep, *refs):
    outs, pieces = refs[-4:], refs[:-4]
    each = outs[0].shape[-1]
    at, width = 0, min(256, each)
    for piece in pieces:
        for first in range(0, piece.shape[-1], width):
            total = keep[..., at : at + width] + piece[..., first : first + width]
            right, place = divmod(at, each)
            for side in range(2):
                outs[side + 2 * right][..., place : place + width] = (
                    total[:, side] if mixed and right else total[:, :, side]
                )
            at += width


def sum_first(keep, coming, mixed, deps=()):
    lead, (tokens, width) = keep.shape[:-2], keep.shape[-2:]
    chunk = min(32, tokens)
    four = lambda j: (0, 0, j, 0)
    five = lambda j: (0, 0, 0, j, 0)
    outs = 4
    each = 2 * width // outs
    return call(
        functools.partial(first_kernel, mixed),
        (tokens // chunk,),
        [pl.BlockSpec(lead + (chunk, value.shape[-1]), five) for value in [keep] + coming],
        [pl.BlockSpec(lead[:2] + (chunk, each), four)] * outs,
        [jax.ShapeDtypeStruct(lead[:2] + (tokens, each), BF)] * outs,
        [],
        0,
        0,
        deps,
        prefetch=0,
    )(keep, *coming)


def last_kernel(*refs):
    width = refs[0].shape[1]
    for i in range(len(refs) // 2):
        refs[-1][:, i * width : (i + 1) * width] = refs[2 * i][...] + refs[2 * i + 1][...]


def last_sum(kept, coming, deps=()):
    tokens, width = kept[0].shape
    spec = pl.BlockSpec((tokens, width), lambda j: (0, 0))
    count = len(kept)
    return call(
        last_kernel,
        (1,),
        [spec] * (2 * count),
        pl.BlockSpec((tokens, count * width), lambda j: (0, 0)),
        jax.ShapeDtypeStruct((tokens, count * width), BF),
        [],
        0,
        0,
        deps,
        prefetch=0,
    )(*[value for pair in zip(kept, coming) for value in pair])


def join_kernel(axes, cut, *refs):
    count = len(axes)
    held = 2 if cut else 2 * count
    outs, stages = refs[held : held + count], refs[held + count : held + 2 * count]
    in_sems, out_sems = refs[held + 2 * count :]
    reads, writes = [], []
    for i, axis in enumerate(axes):
        width = outs[i].shape[-1]
        for side in range(2):
            n = 2 * i + side
            at = (slice(None),) * axis + (slice(side, side + 1),)
            source = refs[side].at[..., i * width : (i + 1) * width] if cut else refs[n]
            reads.append(pltpu.make_async_copy(source, stages[i].at[at], in_sems.at[n]))
            writes.append(
                pltpu.make_async_copy(stages[i].at[at], outs[i].at[at], out_sems.at[n])
            )
    for copy in reads:
        copy.start()
    for read, write in zip(reads, writes):
        read.wait()
        write.start()
    for copy in writes:
        copy.wait()


def join(now, coming, axes, deps=(), cut=False):
    out_shape, operands = [], []
    for value, other in zip(now, coming):
        operands += [value, other]
    for i, axis in enumerate(axes):
        value = now[0 if cut else i]
        shape = value.shape[:axis] + (2,) + value.shape[axis + 1 : -1]
        width = value.shape[-1] // (2 if cut else 1)
        out_shape.append(jax.ShapeDtypeStruct(shape + (width,), BF))
    place = pl.BlockSpec(memory_space=pl.ANY)
    return call(
        functools.partial(join_kernel, tuple(axes), cut),
        (),
        [place] * len(operands),
        [place] * len(out_shape),
        out_shape,
        [pltpu.VMEM(whole.shape, BF) for whole in out_shape]
        + [pltpu.SemaphoreType.DMA((2 * len(axes),))] * 2,
        0,
        0,
        deps,
        prefetch=0,
    )(*operands)


def hidden_kernel(kept, coming, prob, out):
    gate = kept[0].astype(F32) + coming[0].astype(F32)
    up = kept[1].astype(F32) + coming[1].astype(F32)
    out[...] = (gate * jax.nn.sigmoid(gate) * up * prob[...]).astype(BF)


def slopes_kernel(kept, coming, prob, grad_kept, grad_coming, out):
    gate = kept[0].astype(F32) + coming[0].astype(F32)
    up = kept[1].astype(F32) + coming[1].astype(F32)
    grad = (grad_kept[0].astype(F32) + grad_coming[0].astype(F32)) * prob[...]
    sigma = jax.nn.sigmoid(gate)
    out[0] = (grad * up * sigma * (1.0 + gate * (1.0 - sigma))).astype(BF)
    out[1] = (grad * gate * sigma).astype(BF)


def by_rows(kernel, operands, stacks, outs, deps=()):
    rows, hidden = operands[0].shape[1:]
    chunk = rows // 2 if rows % 32 == 0 else rows
    return call(
        kernel,
        (rows // chunk,),
        [
            pl.BlockSpec((chunk, 1), lambda j: (j, 0))
            if value.ndim == 2
            else pl.BlockSpec((value.shape[0], chunk, hidden), lambda j: (0, j, 0))
            for value in operands
        ],
        [pl.BlockSpec((2, chunk, hidden), lambda j: (0, j, 0))] * stacks
        + [pl.BlockSpec((chunk, hidden), lambda j: (j, 0))] * outs,
        [jax.ShapeDtypeStruct((2, rows, hidden), BF)] * stacks
        + [jax.ShapeDtypeStruct((rows, hidden), BF)] * outs,
        [],
        0,
        0,
        deps,
        prefetch=0,
    )(*operands)


def nothing_kernel(*refs):
    pass


def after(value, *others):
    return pl.pallas_call(
        nothing_kernel,
        in_specs=[pl.BlockSpec(memory_space=pl.ANY)] * (1 + len(others)),
        out_specs=pl.BlockSpec(memory_space=pl.ANY),
        out_shape=jax.ShapeDtypeStruct(value.shape, value.dtype),
        input_output_aliases={0: 0},
    )(value, *others)


def fast(tokens, routing, gate_probs, paired, w_gate, w_up, w_down, cotangent):
    n_expert = lax.axis_size("expert")
    token_count, top_count = routing.shape
    slab = tokens.shape[1]
    hidden = w_gate.shape[2]
    capacity = max(2, 5 * token_count * top_count // (4 * n_expert))
    half = slab // 2
    mine = n_expert // 2
    copy = lax.axis_index("expert")
    dp = lax.axis_index("dp").astype(jnp.int32)
    dp_one = dp.reshape(1)
    other_one = (1 - dp).reshape(1)
    gate_slab, up_slab, down_slab = w_gate[0], w_up[0], w_down[0]

    def cross(value, bit):
        return exchange(value, "expert", bit)

    meta = jnp.concatenate([routing.astype(BF)] + split_exact(gate_probs), axis=1)
    meta = jnp.pad(meta, ((0, 0), (0, 128 - meta.shape[1])))

    def blocks(value):
        return [value[:, :half].reshape(1, 1, 1, token_count, half), value[:, half:].reshape(1, 1, 1, token_count, half)]

    def widen(now, bits, coming=None, deps=()):
        if coming is None:
            coming = [cross(value, bit) for value, bit in zip(now, bits)]
        axis = {8: 0, 4: 1, 2: 2}
        return join(now, coming, [axis[bit] for bit in bits], deps)

    token_now = blocks(tokens)
    token_now[0] = jnp.concatenate([token_now[0], meta.reshape(1, 1, 1, token_count, -1)], axis=-1)
    token_now = widen(token_now, (8, 8))
    token_now = widen(token_now, (4, 2))
    token_now = widen(token_now, (2, 4))
    cot_whole = cotangent.reshape(1, 1, 1, token_count, slab)

    def finish(now):
        pieces = []
        for value in now:
            value = value.reshape(mine, token_count, -1)
            pieces += [value, cross(value, 1)]
        return pieces

    token_pieces = finish(token_now)

    meta = jnp.stack([piece[:, :, half:] for piece in token_pieces[:2]], axis=1)
    meta = meta.reshape(n_expert, token_count, -1).astype(F32)
    named, high, middle, low = [
        meta[:, :, i * top_count : (i + 1) * top_count] for i in range(4)
    ]
    probs = high + middle + low
    before = (
        jnp.arange(token_count)[:, None] < jnp.arange(token_count)[None, :]
    ).astype(BF)

    def selection(index):
        hit = named == index.astype(F32)
        member = jnp.any(hit, axis=2)
        slot = product(member.astype(BF), before).astype(jnp.int32)
        return hit, jnp.where(member, slot, -1)

    hit, slots = selection(copy)
    _, pair_slots = selection(jnp.bitwise_xor(copy, mine))
    pair_slots = jnp.where(paired[0] == 1, pair_slots, -1)
    select = jnp.arange(capacity, dtype=jnp.int32)[None, :, None] == slots[:, None, :]
    shift = capacity * (jnp.arange(n_expert, dtype=jnp.int32) % 2)[:, None]
    slots, pair_slots = [
        jnp.where(value < 0, value, value + shift) for value in (slots, pair_slots)
    ]
    columns, pair_columns = slots[:, :, None], pair_slots[:, :, None]
    prob = jnp.sum(jnp.where(hit, probs, 0.0), axis=2)
    row_prob = jnp.sum(jnp.where(select, prob[:, None, :], 0.0), axis=2)
    prob_own = lax.dynamic_slice_in_dim(row_prob, dp * mine, mine).reshape(mine * capacity, 1)

    def rows_of(which, pieces, weights, dims, *deps):
        return rows_product(which, slots, pieces, weights, dims, capacity, half, deps)[0]

    def over(value):
        return exchange(value, "dp", 1)

    leaving = rows_of(other_one, token_pieces, [gate_slab, up_slab], NN)
    coming = over(leaving)
    cot_now = join([cot_whole], [cross(cot_whole, 8)], (0, 0), (leaving,), True)
    kept = rows_of(dp_one, token_pieces, [gate_slab, up_slab], NN, cot_now[0])
    cot_now = widen(cot_now, (4, 2), None, (kept,))
    cot_third = [cross(value, bit) for value, bit in zip(cot_now, (2, 4))]
    (hid,) = by_rows(hidden_kernel, [kept, coming, prob_own], 0, 1)
    hid_crossed = cross(hid, mine)
    hid_other = over(hid)
    cot_pieces = finish(widen(cot_now, (2, 4), cot_third, (hid,)))
    leaving = rows_of(other_one, cot_pieces, [down_slab], NT)
    dhid_coming = over(leaving)
    dhid_kept = rows_of(dp_one, cot_pieces, [down_slab], NT)
    out_keep, *out_send = back_product(
        dp_one, columns, [hid, hid_other], [down_slab], NN, capacity, OUT_PARTS, (dhid_kept, leaving)
    )
    (slopes,) = by_rows(
        slopes_kernel,
        [kept, coming, prob_own, dhid_kept, dhid_coming],
        1,
        0,
        (out_send[0], hid_crossed),
    )
    slopes_other = over(slopes)
    slopes_crossed = cross(slopes, mine)

    shape = (2, 2, 2, token_count, slab)

    def first_sum(keep, send, mixed, *deps):
        coming = [cross(value, 1).reshape(shape[:-1] + value.shape[-1:]) for value in send]
        return sum_first(keep.reshape(shape), coming, mixed, deps)

    def next_sum(parts, bits, axis, *deps):
        kept, sent = parts[::2], parts[1::2]
        coming = [cross(value, bit) for value, bit in zip(sent, bits)]
        return sum_split(kept, coming, [axis] * len(kept), axis == 0, deps)

    def end_sum(parts, *deps):
        return last_sum(parts[::2], [cross(value, 8) for value in parts[1::2]], deps)

    def gradient(values, pieces, flat, *deps):
        return weight_gradient(
            dp_one, columns, pair_columns, values, pieces, flat, capacity, half, deps
        )

    out_parts = first_sum(out_keep, out_send, MIXED_OUT)
    out_bits = ((2, 4), (4, 2)) if MIXED_OUT else ((2, 2), (4, 4))
    back_bits = ((2, 4), (4, 2)) if MIXED else ((2, 2), (4, 4))
    back_keep, *back_send = back_product(
        dp_one,
        columns,
        [(slopes, 0), (slopes_other, 0), (slopes, 1), (slopes_other, 1)],
        [gate_slab, up_slab],
        NT,
        capacity,
        BACK_PARTS,
        (out_parts[1],),
    )
    hid_beyond = over(hid_crossed)
    out_parts = next_sum(out_parts, out_bits[0], 1, back_keep)
    back_send[1] = after(back_send[1], out_parts[1])
    back_parts = list(first_sum(back_keep, back_send, MIXED))
    back_parts[3] = after(back_parts[3], slopes_crossed, hid_beyond)
    slopes_beyond = [over(slopes_crossed[part]) for part in range(2)]

    def slope_values(part):
        stacks = [(value, part) for value in (slopes, slopes_other, slopes_crossed)]
        return stacks + [slopes_beyond[part]]

    out_parts = next_sum(out_parts, out_bits[1], 0, back_parts[3])
    grad_down = gradient(
        [hid, hid_other, hid_crossed, hid_beyond], cot_pieces, False, out_parts[1]
    )
    output = end_sum(out_parts, grad_down)
    back_parts = next_sum(back_parts, back_bits[0], 1, output)
    grad_gate = gradient(slope_values(0), token_pieces, True, back_parts[1])
    back_parts = next_sum(back_parts, back_bits[1], 0, grad_gate)
    grad_up = gradient(slope_values(1), token_pieces, True, back_parts[1])
    grad_tokens = end_sum(back_parts)
    return (output, grad_tokens, grad_gate[None], grad_up[None], grad_down[None])


def per_device(*arrays):
    quick = lax.axis_size("dp") == 2 and lax.axis_size("expert") == 16
    return (fast if quick else general)(*arrays)


def solution(mesh):
    return jax.shard_map(
        per_device,
        mesh=mesh,
        in_specs=(
            P("expert", "dp"),
            P("expert", None),
            P("expert", None),
            P("expert"),
            P("expert", "dp", None),
            P("expert", "dp", None),
            P("expert", None, "dp"),
            P("expert", "dp"),
        ),
        out_specs=(
            P("expert", "dp"),
            P("expert", "dp"),
            P("expert", "dp", None),
            P("expert", "dp", None),
            P("expert", None, "dp"),
        ),
        check_vma=False,
    )
```
